256 devices in a mesh: gx: 16 (over x, z_lo), gy: 16 (over z_hi, y, core).
Axes of the slice: x: 4, y: 4, z: 8 (z_hi: 2, z_lo: 4; z = z_hi * 4 + z_lo), core: 2. Of those that a mesh axis runs over, the one named last changes fastest.
Arguments:
- ensemble: bfloat16 [128, 128, 64, 128], P('gx', 'gy'), may hold values from -6 to 6
- obs_anom: bfloat16 [16, 16, 128, 128], P('gx', 'gy'), may hold values from -7 to 7
- obs_innov: bfloat16 [16, 16, 128], P('gx', 'gy'), may hold values from -8 to 8
- obs_prec: bfloat16 [16, 16, 128], P('gx', 'gy'), may hold values from 0.099609375 to 2
- obs_pos: int32 [16, 16, 2, 128], P('gx', 'gy'), may hold values from 0 to 7
- obs_count: int32 [16, 16], P('gx', 'gy'), may hold values from 16 to 128, as said below
Outputs:
- analysis: bfloat16 [128, 128, 64, 128], P('gx', 'gy')
The draws below stay inside these ranges and needn't reach their ends.
Inputs may be any that keep to these rules, and one draw needn't show every extreme that they name: `obs_count`: some tile holds exactly the most and some tile exactly the least.
All inputs are finite; a program needn't handle non-finite values.
Results may differ from the reference program's by a relative error of at most 0.0022.
The reference program's roundings to bfloat16 on the way count: a program that leaves them out, or rounds other values in their place, can miss the bound.
Values may be sent and summed in bfloat16 or wider, within the bound.
No kernel may reach another device: no remote copies, remote signals or barrier semaphores. Data moves between devices by JAX's collectives and lax.ppermute only.
A program may use at most 128 MiB of HBM per device.

```python
import math
import jax
import jax.numpy as jnp
import numpy as np
from jax import lax

K = 128
NVAR = 64
CT = 8
OBS = 128
APX = 4
ITERS = 4
TILES_X = 16
TILES_Y = 16
NX = 128
NY = 128
SPACING = 2
NHALF = 32
RLOC = 12


def draw_obs_anom(key, part):
    key = jax.random.fold_in(key, 11)
    base_key = jax.random.fold_in(key, 0)
    full_shape = (TILES_X, TILES_Y, OBS, K)
    base_draw = jnp.clip(jax.random.normal(base_key, full_shape, jnp.float32), -4.0, 4.0)
    values = 0.8 * (base_draw + 0.7 * jnp.roll(base_draw, 1, axis=3))
    return values.astype(jnp.bfloat16)


def draw_obs_count(key, part):
    key = jax.random.fold_in(key, 23)
    count_key, full_key, least_key = jax.random.split(key, 3)
    tile_total = TILES_X * TILES_Y
    counts = jax.random.randint(count_key, (TILES_X, TILES_Y), OBS // 8, OBS + 1)
    chosen = jax.random.randint(full_key, (), 0, tile_total)
    second = (chosen + 1 + jax.random.randint(least_key, (), 0, tile_total - 1)) % tile_total
    flat_index = jnp.arange(tile_total, dtype=jnp.int32).reshape(TILES_X, TILES_Y)
    counts = jnp.where(flat_index == chosen, OBS, counts)
    counts = jnp.where(flat_index == second, OBS // 8, counts)
    return counts.astype(jnp.int32)


def plant(entries, stream_key, low, largest):
    place = [jax.random.randint(jax.random.fold_in(stream_key, axis), (), 0, length) for axis, length in enumerate(entries.shape)]
    longest = entries.shape.index(max(entries.shape))
    neighbour = place[:longest] + [(place[longest] + 1) % entries.shape[longest]] + place[longest + 1:]
    return entries.at[tuple(place)].set(low).at[tuple(neighbour)].set(largest)


def steps_of(key, shape, shards, least, largest):
    gain = 1.0
    for axis_at, parts in shards:
        steps = jax.random.uniform(jax.random.fold_in(jax.random.fold_in(key, 6), axis_at), (parts,), jnp.float32, least / len(shards), largest / len(shards))
        gain = gain * jnp.repeat(jnp.exp(steps), shape[axis_at] // parts).reshape((-1,) + (1,) * (len(shape) - 1 - axis_at))
    return gain


def scatter_about(own_key, shape, deviation, most, pieces=(), held_as=jnp.bfloat16):
    result = deviation * jax.random.normal(own_key, shape, jnp.float32)
    if pieces:
        result = result * steps_of(own_key, shape, pieces, -0.22, 0.18)
    return jnp.clip(result, -most, most).astype(held_as)


def setup_inputs(seed: int = 0) -> dict:
    keys = jax.random.split(jax.random.key(seed), 7)
    ensemble = scatter_about(keys[0], (NX, NY, NVAR, K), 1.0, 6.0, ((0, 16), (1, 16)))
    obs_anom = draw_obs_anom(jax.random.fold_in(keys[6], 71), 0)
    obs_innov = scatter_about(keys[2], (TILES_X, TILES_Y, OBS), 2.0, 8.0, ((0, 16), (1, 16)))
    obs_prec = jnp.clip(jnp.exp(math.log(2.0) - 2.9996462 * jax.random.uniform(keys[3], (TILES_X, TILES_Y, OBS), jnp.float32) ** steps_of(keys[3], (TILES_X, TILES_Y, OBS), ((0, 16), (1, 16)), -0.2, 0.2)), 0.099609375, 2.0).astype(jnp.bfloat16)
    obs_pos = plant(jax.random.randint(keys[4], (TILES_X, TILES_Y, 2, OBS), 0, CT), jax.random.fold_in(keys[4], 1), 0, CT - 1).astype(jnp.int32)
    obs_count = draw_obs_count(jax.random.fold_in(keys[6], 71), 0)
    return {"ensemble": ensemble, "obs_anom": obs_anom, "obs_innov": obs_innov, "obs_prec": obs_prec, "obs_pos": obs_pos, "obs_count": obs_count}


exact_mode = lax.Precision.HIGHEST

def localize(sq_dist, radius):
    inside = sq_dist < radius * radius
    wave_rate = jnp.exp(-sq_dist * (2.0 / (radius * radius)))
    ocean_rate = jnp.exp(-sq_dist * (4.5 / (radius * radius)))
    stacked = jnp.stack([wave_rate, ocean_rate], axis=-2)
    return jnp.where(inside[..., None, :], stacked, jnp.zeros_like(stacked))

def point_coords(spacing, point_count):
    return spacing * jnp.arange(point_count, dtype=jnp.float32) + (spacing - 1) / 2.0

def inverse_root(system, sweeps):
    identity = jnp.eye(system.shape[-1], dtype=system.dtype)
    norm_value = jnp.sqrt(lax.optimization_barrier(jnp.sum(system * system, axis=(-2, -1))))
    root_iter = system / norm_value[..., None, None]
    inv_iter = jnp.broadcast_to(identity, system.shape)
    for sweep_index in range(sweeps):
        half_step = 0.5 * (3.0 * identity - jnp.einsum('pij,pjk->pik', inv_iter, root_iter, precision=exact_mode))
        new_root = jnp.einsum('pij,pjk->pik', root_iter, half_step, precision=exact_mode)
        new_inv = jnp.einsum('pij,pjk->pik', half_step, inv_iter, precision=exact_mode)
        root_iter, inv_iter = (new_root, new_inv)
    return (inv_iter, norm_value)

def make_transforms(gram, pull, members):
    system = jnp.eye(members, dtype=gram.dtype) + gram / (members - 1.0)
    inv_iter, norm_value = inverse_root(system, ITERS)
    inner_vec = jnp.einsum('pij,pj->pi', inv_iter, pull, precision=exact_mode)
    shift_vec = jnp.einsum('pij,pj->pi', inv_iter, inner_vec, precision=exact_mode) / (norm_value[:, None] * (members - 1.0))
    matrix = inv_iter / jnp.sqrt(norm_value)[:, None, None] + shift_vec[:, :, None]
    return matrix.astype(jnp.bfloat16)

def tile_transforms(anom_seen, innov_seen, prec_seen, rel_x, rel_y):
    centers = point_coords(SPACING, APX)
    diff_x = rel_x[None, :] - centers[:, None]
    diff_y = rel_y[None, :] - centers[:, None]
    sq_dist = diff_x[:, None, :] ** 2 + diff_y[None, :, :] ** 2
    weights = localize(sq_dist, RLOC) * prec_seen
    flat_w = weights.reshape(-1, weights.shape[-1])
    anom_wide = anom_seen.astype(jnp.float32)
    scaled = lax.optimization_barrier((jnp.sqrt(flat_w)[:, :, None] * anom_wide[None]).astype(jnp.bfloat16))
    scaled = scaled.astype(jnp.float32)
    gram = jnp.einsum('pok,pol->pkl', scaled, scaled, precision=exact_mode)
    pull = jnp.dot(flat_w * innov_seen[None, :], anom_wide, precision=exact_mode)
    return make_transforms(gram, pull, K)

def apply_weights(local, mean_tile, extended, corner_w):
    half_rim = SPACING // 2
    quad_count = APX + 1
    padded = jnp.pad(local, ((half_rim, half_rim), (half_rim, half_rim), (0, 0), (0, 0)))
    blocks = padded.reshape(quad_count, SPACING, quad_count, SPACING, 2, NHALF, K).astype(jnp.float32)
    total = jnp.zeros(blocks.shape, jnp.float32)
    for corner_x in range(2):
        for corner_y in range(2):
            matrices = extended[corner_x:corner_x + quad_count, corner_y:corner_y + quad_count].astype(jnp.float32)
            product = jnp.einsum('qrpsgvk,qpgkl->qrpsgvl', blocks, matrices, precision=exact_mode)
            scale_xy = corner_w[corner_x][None, :, None, None, None, None, None] * corner_w[corner_y][None, None, None, :, None, None, None]
            total = total + product * scale_xy
    total = total.reshape(quad_count * SPACING, quad_count * SPACING, NVAR, K)[half_rim:half_rim + CT, half_rim:half_rim + CT]
    return (mean_tile[..., None] + total).astype(jnp.bfloat16)

def reference(ensemble, obs_anom, obs_innov, obs_prec, obs_pos, obs_count):
    ensemble_mean = lax.optimization_barrier(jnp.sum(ensemble.astype(jnp.float32), axis=-1)) / K
    anomalies = (ensemble.astype(jnp.float32) - ensemble_mean[..., None]).astype(jnp.bfloat16)
    slot_index = jnp.arange(OBS, dtype=jnp.int32)
    live_slot = (slot_index[None, None, :] < obs_count[:, :, None]).astype(jnp.float32)
    prec_live = obs_prec.astype(jnp.float32) * live_slot
    shift_x = jnp.asarray(np.repeat(np.arange(-2, 3), 5), dtype=jnp.int32)
    shift_y = jnp.asarray(np.tile(np.arange(-2, 3), 5), dtype=jnp.int32)

    def per_tile(flat_tile):
        tile_x = flat_tile // TILES_Y
        tile_y = flat_tile % TILES_Y
        source_x = (tile_x + shift_x) % TILES_X
        source_y = tile_y + shift_y
        valid_row = ((source_y >= 0) & (source_y < TILES_Y)).astype(jnp.float32)
        clamp_y = jnp.clip(source_y, 0, TILES_Y - 1)
        anom_seen = obs_anom[source_x, clamp_y].reshape(-1, K)
        innov_seen = obs_innov[source_x, clamp_y].astype(jnp.float32).reshape(-1)
        prec_seen = (prec_live[source_x, clamp_y] * valid_row[:, None]).reshape(-1)
        pos_seen = obs_pos[source_x, clamp_y].astype(jnp.float32)
        rel_x = (pos_seen[:, 0, :] + (shift_x * CT).astype(jnp.float32)[:, None]).reshape(-1)
        rel_y = (pos_seen[:, 1, :] + (shift_y * CT).astype(jnp.float32)[:, None]).reshape(-1)
        return tile_transforms(anom_seen, innov_seen, prec_seen, rel_x, rel_y)
    tile_ids = jnp.arange(TILES_X * TILES_Y, dtype=jnp.int32)
    tile_mats = lax.map(per_tile, tile_ids)
    point_grid = tile_mats.reshape(TILES_X, TILES_Y, APX, APX, 2, K, K).transpose(0, 2, 1, 3, 4, 5, 6)
    point_grid = point_grid.reshape(TILES_X * APX, TILES_Y * APX, 2, K, K)
    frac_cell = (jnp.arange(SPACING, dtype=jnp.float32) + 0.5) / SPACING
    corner_w = jnp.stack([1.0 - frac_cell, frac_cell])

    def apply_tile(flat_tile):
        tile_x = flat_tile // TILES_Y
        tile_y = flat_tile % TILES_Y
        ext_x = (tile_x * APX - 1 + jnp.arange(APX + 2, dtype=jnp.int32)) % (TILES_X * APX)
        ext_y = jnp.clip(tile_y * APX - 1 + jnp.arange(APX + 2, dtype=jnp.int32), 0, TILES_Y * APX - 1)
        extended = point_grid[ext_x][:, ext_y]
        zero_index = jnp.zeros((), jnp.int32)
        start_x = (tile_x * CT).astype(jnp.int32)
        start_y = (tile_y * CT).astype(jnp.int32)
        local = lax.dynamic_slice(anomalies, (start_x, start_y, zero_index, zero_index), (CT, CT, NVAR, K))
        mean_tile = lax.dynamic_slice(ensemble_mean, (start_x, start_y, zero_index), (CT, CT, NVAR))
        return apply_weights(local, mean_tile, extended, corner_w)
    tiles_out = lax.map(apply_tile, tile_ids)
    tiles_out = tiles_out.reshape(TILES_X, TILES_Y, CT, CT, NVAR, K).transpose(0, 2, 1, 3, 4, 5)
    return tiles_out.reshape(NX, NY, NVAR, K)
```

```python
import functools

import jax
import jax.numpy as jnp
from jax import lax
from jax.experimental import pallas as pl
from jax.experimental.pallas import tpu as pltpu
from jax.sharding import PartitionSpec as P

K = 128
APX = 4
CT = 8
SPACING = 2
RLOC = 12
NHALF = 32
ROWS = K + 16
VMEM = 50 << 20

NT = (((1,), (1,)), ((), ()))
NN = (((1,), (0,)), ((), ()))
F32 = jnp.float32
BF16 = jnp.bfloat16


def center(a):
    return SPACING * a + (SPACING - 1) / 2.0


def least_distance(offset, point):
    return min(abs(offset * CT + s - center(point)) for s in range(CT))


def tiles_of(point):
    a, b = point
    return [
        (ox, oy)
        for oy in range(-2, 3)
        for ox in range(-2, 3)
        if least_distance(ox, a) ** 2 + least_distance(oy, b) ** 2 < RLOC * RLOC
    ]


def split(x):
    hi = x.astype(BF16)
    lo = (x - hi.astype(F32)).astype(BF16)
    return hi, lo


def mm(a, b):
    left = jnp.concatenate([a[0], a[1]], 1)
    right = jnp.concatenate([b[0], b[1]], 1)
    right = jnp.concatenate([right, right], 0)
    out = lax.dot_general(left, right, NN, preferred_element_type=F32)
    return out[:, :K] + out[:, K:]


C0, C1, C2, C3, C4 = 2.25, -2.4375, 1.6875, -0.5625, 0.0625


def two_steps(xs, parts, eye):
    n = range(len(xs))
    sq = [mm(parts[i], parts[i]) for i in n]
    high = [mm(split(sq[i]), split(C3 * xs[i] + C4 * sq[i])) for i in n]
    return [C0 * eye + C1 * xs[i] + C2 * sq[i] + high[i] for i in n]


def four_steps(xs, eye):
    n = range(len(xs))
    x_parts = [split(x) for x in xs]
    z = two_steps(xs, x_parts, eye)
    z_parts = [split(v) for v in z]
    z_sq = [mm(z_parts[i], z_parts[i]) for i in n]
    m = [mm(x_parts[i], split(z_sq[i])) for i in n]
    q = two_steps(m, [split(v) for v in m], eye)
    return [mm(z_parts[i], split(q[i])) for i in n]


def pack_kernel(count_ref, anom_ref, innov_ref, prec_ref, pos_ref, out_ref):
    out_ref[0:K, :] = anom_ref[...].astype(F32).T.astype(BF16)
    slot = lax.broadcasted_iota(jnp.int32, (1, K), 1)
    live = jnp.where(slot < count_ref[0, 0], prec_ref[...].astype(F32), 0.0)
    meta = jnp.concatenate(
        [innov_ref[...].astype(F32), live, pos_ref[...].astype(F32), jnp.zeros((12, K), F32)], 0
    )
    out_ref[K:ROWS, :] = meta.astype(BF16)


def point_weights(meta, ox, oy, points):
    rows = (len(points) + 7) // 8 * 8
    at = lax.broadcasted_iota(jnp.int32, (rows, K), 0)
    px = jnp.zeros((rows, K), F32)
    py = px
    for i, (a, b) in enumerate(points):
        px = jnp.where(at == i, center(a), px)
        py = jnp.where(at == i, center(b), py)
    dx = (meta[2:3] + float(ox * CT)) - px
    dy = (meta[3:4] + float(oy * CT)) - py
    sq = dx * dx + dy * dy
    inside = sq < float(RLOC * RLOC)
    out = []
    for rate in (2.0, 4.5):
        out.append(jnp.where(inside, jnp.exp(-sq * (rate / (RLOC * RLOC))), 0.0) * meta[1:2])
    return out


def points_kernel(points, batch, *refs):
    x_refs, y_refs = refs[0:5], refs[5:9]
    out_ref, sw_ref, wp_ref, s_ref, g_ref, pull_ref = refs[9:]

    def block(t):
        ox, oy = t
        if oy == 0:
            return x_refs[ox + 2]
        wide = abs(oy) == 1
        ref = y_refs[{-1: 0, 1: 1, -2: 2, 2: 3}[oy]]
        return ref.at[ox + 2 if wide else ox + 1]

    seen = sorted({t for p in points for t in tiles_of(p)})
    place = {t: i for i, t in enumerate(seen)}
    rows = (len(points) + 7) // 8 * 8
    for t in seen:
        meta = block(t)[K:ROWS, :].astype(F32)
        w = point_weights(meta, t[0], t[1], points)
        lanes = slice(place[t] * K, place[t] * K + K)
        for g in range(2):
            sw_ref[place[t], g * rows : g * rows + rows, :] = jnp.sqrt(w[g])
        hi, lo = split(jnp.concatenate(w, 0) * meta[0:1])
        wp_ref[0 : 2 * rows, lanes] = hi
        wp_ref[2 * rows : 4 * rows, lanes] = lo
    anom_seen = jnp.concatenate([block(t)[0:K, :] for t in seen], 1)
    pull = lax.dot_general(
        anom_seen, wp_ref[:, 0 : len(seen) * K], NT, preferred_element_type=F32
    )
    pull_ref[...] = pull[:, 0 : 2 * rows] + pull[:, 2 * rows : 4 * rows]

    for i, p in enumerate(points):
        own = tiles_of(p)
        for j, t in enumerate(own):
            anom = block(t)[0:K, :].astype(F32)
            for g in range(2):
                scale = sw_ref[place[t], g * rows + i : g * rows + i + 1, :]
                s_ref[i % 2, g, :, j * K : j * K + K] = (anom * scale).astype(BF16)
        width = len(own) * K
        for g in range(2):
            s = s_ref[i % 2, g, :, 0:width]
            g_ref[2 * i + g] = lax.dot_general(s, s, NT, preferred_element_type=F32)

    row = lax.broadcasted_iota(jnp.int32, (K, K), 0)
    col = lax.broadcasted_iota(jnp.int32, (K, K), 1)
    eye = jnp.where(row == col, 1.0, 0.0).astype(F32)
    total = 2 * len(points)
    for first in range(0, total, batch):
        ids = range(first, min(first + batch, total))
        xs, norms = [], []
        for i in ids:
            system = eye + g_ref[i] * (1.0 / (K - 1.0))
            sq = jnp.sum(jnp.sum(system * system, 0, keepdims=True), 1, keepdims=True)
            norm = jnp.sqrt(sq)
            norms.append(norm)
            xs.append(system * (1.0 / norm))
        zs = four_steps(xs, eye)
        for i, z, norm in zip(ids, zs, norms):
            lane = (i % 2) * rows + i // 2
            inner = jnp.sum(z * pull_ref[:, lane : lane + 1], 0, keepdims=True)
            shift = jnp.sum(z * inner, 1, keepdims=True) * (1.0 / (norm * (K - 1.0)))
            out_ref[i // 2, i % 2] = (z * (1.0 / jnp.sqrt(norm)) + shift).astype(BF16)


def transforms(points, x_blocks, y_blocks, batch, name):
    rows = (len(points) + 7) // 8 * 8
    seen = len({t for p in points for t in tiles_of(p)})
    most = max(len(tiles_of(p)) for p in points)
    n = len(points)
    return pl.pallas_call(
        functools.partial(points_kernel, points, batch),
        out_shape=jax.ShapeDtypeStruct((n, 2, K, K), BF16),
        scratch_shapes=[
            pltpu.VMEM((seen, 2 * rows, K), F32),
            pltpu.VMEM((4 * rows, seen * K), BF16),
            pltpu.VMEM((2, 2, K, most * K), BF16),
            pltpu.VMEM((2 * n, K, K), F32),
            pltpu.VMEM((K, 2 * rows), F32),
        ],
        compiler_params=pltpu.CompilerParams(vmem_limit_bytes=VMEM),
        cost_estimate=pl.CostEstimate(
            flops=n * 1_400_000_000 // 2, bytes_accessed=4_000_000, transcendentals=0
        ),
        name=name,
    )(*x_blocks, *y_blocks)


def apply_kernel(edge_ref, ens_ref, own_ref, low_ref, high_ref, out_ref, rim_ref):
    for side, (src, own) in enumerate(((low_ref, 0), (high_ref, APX - 1))):

        @pl.when(edge_ref[side] != 0)
        def _():
            rim_ref[side] = own_ref[own]

        @pl.when(edge_ref[side] == 0)
        def _():
            rim_ref[side] = src[...]

    def transform(x, y, g):
        if y == 0:
            return rim_ref[0, x, g]
        if y == APX + 1:
            return rim_ref[1, x, g]
        return own_ref[y - 1, x, g]

    ones = jnp.ones((K, K), BF16)
    frac = [(s + 0.5) / SPACING for s in range(SPACING)]
    corner = [[1.0 - f for f in frac], frac]
    for q in range(APX + 1):
        for p in range(APX + 1):
            cells = [
                (s, t)
                for s in range(2)
                for t in range(2)
                if 0 <= 2 * q - 1 + s < CT and 0 <= 2 * p - 1 + t < CT
            ]
            ens = jnp.concatenate([ens_ref[2 * q - 1 + s, 2 * p - 1 + t] for s, t in cells], 0)
            mean = lax.dot_general(ens, ones, NN, preferred_element_type=F32) * (1.0 / K)
            anom = (ens.astype(F32) - mean).astype(BF16)
            for g in range(2):
                spans = [slice(c * 2 * NHALF + g * NHALF, c * 2 * NHALF + (g + 1) * NHALF) for c in range(len(cells))]
                left = jnp.concatenate([anom[sp] for sp in spans], 0)
                sums = [mean[sp] for sp in spans]
                adds = [None] * len(cells)
                for cx in range(2):
                    for cy in range(2):
                        prod = lax.dot_general(
                            left, transform(q + cx, p + cy, g), NN, preferred_element_type=F32
                        )
                        for c, (s, t) in enumerate(cells):
                            term = prod[c * NHALF : (c + 1) * NHALF] * (corner[cx][s] * corner[cy][t])
                            adds[c] = term if adds[c] is None else adds[c] + term
                for c, (s, t) in enumerate(cells):
                    out_ref[2 * q - 1 + s, 2 * p - 1 + t, g * NHALF : (g + 1) * NHALF, :] = (
                        sums[c] + adds[c]
                    ).astype(BF16)


def apply(edges, ensemble, own, low, high):
    return pl.pallas_call(
        apply_kernel,
        out_shape=jax.ShapeDtypeStruct(ensemble.shape, BF16),
        in_specs=[pl.BlockSpec(memory_space=pltpu.SMEM)] + [pl.BlockSpec(memory_space=pltpu.VMEM)] * 4,
        scratch_shapes=[pltpu.VMEM((2, APX + 2, 2, K, K), BF16)],
        compiler_params=pltpu.CompilerParams(vmem_limit_bytes=VMEM),
        name="apply_transforms",
    )(edges, ensemble, own, low, high)


def shifted(block, axis, distance, closed):
    n = lax.axis_size(axis)
    pairs = [((i + distance) % n, i) for i in range(n) if closed or 0 <= i + distance < n]
    return lax.ppermute(block, axis, pairs)


def shards(ensemble, obs_anom, obs_innov, obs_prec, obs_pos, obs_count):
    own = pl.pallas_call(
        pack_kernel,
        out_shape=jax.ShapeDtypeStruct((ROWS, K), BF16),
        in_specs=[pl.BlockSpec(memory_space=pltpu.SMEM)] + [pl.BlockSpec(memory_space=pltpu.VMEM)] * 4,
        name="pack_slots",
    )(
        obs_count,
        obs_anom.reshape(K, K),
        obs_innov.reshape(1, K),
        obs_prec.reshape(1, K),
        obs_pos.reshape(2, K),
    )
    x_blocks = {0: own}
    for d in (-2, -1, 1, 2):
        x_blocks[d] = shifted(own, "gx", d, True)
    x_list = [x_blocks[d] for d in range(-2, 3)]
    wide = jnp.stack(x_list)
    near = jnp.stack(x_list[1:4])
    y_blocks = [shifted(wide if abs(d) == 1 else near, "gy", d, False) for d in (-1, 1, -2, 2)]
    across = range(-1, APX + 1)
    outer = transforms([(a, b) for b in (0, APX - 1) for a in across], x_list, y_blocks, 12, "outer_points")
    inner = transforms([(a, b) for b in (1, 2) for a in across], x_list, y_blocks, 12, "inner_points")
    outer = outer.reshape(2, APX + 2, 2, K, K)
    inner = inner.reshape(2, APX + 2, 2, K, K)
    low = shifted(outer[1], "gy", -1, False)
    high = shifted(outer[0], "gy", 1, False)
    mats = jnp.concatenate([outer[0:1], inner, outer[1:2]], 0)
    row = lax.axis_index("gy")
    edges = jnp.stack([row == 0, row == lax.axis_size("gy") - 1]).astype(jnp.int32)
    return apply(edges, ensemble, mats, low, high)


def solution(mesh):
    placed = (
        P("gx", "gy", None, None),
        P("gx", "gy", None, None),
        P("gx", "gy", None),
        P("gx", "gy", None),
        P("gx", "gy", None, None),
        P("gx", "gy"),
    )
    return jax.shard_map(
        shards, mesh=mesh, in_specs=placed, out_specs=P("gx", "gy", None, None), check_vma=False
    )
```

```python
import functools

import jax
import jax.numpy as jnp
from jax import lax
from jax.experimental import pallas as pl
from jax.experimental.pallas import tpu as pltpu
from jax.sharding import PartitionSpec as P

K = 128
APX = 4
CT = 8
SPACING = 2
RLOC = 12
NHALF = 32
ROWS = K + 16
VMEM = 50 << 20

NT = (((1,), (1,)), ((), ()))
NN = (((1,), (0,)), ((), ()))
F32 = jnp.float32
BF16 = jnp.bfloat16

POINTS = [(a, b) for b in range(APX) for a in range(-1, APX + 1)]
FIRST = APX + 2


def center(a):
    return SPACING * a + (SPACING - 1) / 2.0


def least_distance(offset, point):
    return min(abs(offset * CT + s - center(point)) for s in range(CT))


def tiles_of(point, rows):
    a, b = point
    return [
        (ox, oy)
        for oy in rows
        for ox in range(-2, 3)
        if least_distance(ox, a) ** 2 + least_distance(oy, b) ** 2 < RLOC * RLOC
    ]


def split(x):
    hi = x.astype(BF16)
    lo = (x - hi.astype(F32)).astype(BF16)
    return hi, lo


def mm(a, b):
    left = jnp.concatenate([a[0], a[1]], 1)
    right = jnp.concatenate([b[0], b[1]], 1)
    right = jnp.concatenate([right, right], 0)
    out = lax.dot_general(left, right, NN, preferred_element_type=F32)
    return out[:, :K] + out[:, K:]


C0, C1, C2, C3, C4 = 2.25, -2.4375, 1.6875, -0.5625, 0.0625


def two_steps(xs, parts, eye):
    n = range(len(xs))
    sq = [mm(parts[i], parts[i]) for i in n]
    high = [mm(split(sq[i]), split(C3 * xs[i] + C4 * sq[i])) for i in n]
    return [C0 * eye + C1 * xs[i] + C2 * sq[i] + high[i] for i in n]


def four_steps(xs, eye):
    n = range(len(xs))
    x_parts = [split(x) for x in xs]
    z = two_steps(xs, x_parts, eye)
    z_parts = [split(v) for v in z]
    z_sq = [mm(z_parts[i], z_parts[i]) for i in n]
    m = [mm(x_parts[i], split(z_sq[i])) for i in n]
    q = two_steps(m, [split(v) for v in m], eye)
    return [mm(z_parts[i], split(q[i])) for i in n]


def pack_kernel(count_ref, anom_ref, innov_ref, prec_ref, pos_ref, out_ref):
    out_ref[0:K, :] = anom_ref[...].astype(F32).T.astype(BF16)
    slot = lax.broadcasted_iota(jnp.int32, (1, K), 1)
    live = jnp.where(slot < count_ref[0, 0], prec_ref[...].astype(F32), 0.0)
    meta = jnp.concatenate(
        [innov_ref[...].astype(F32), live, pos_ref[...].astype(F32), jnp.zeros((12, K), F32)], 0
    )
    out_ref[K:ROWS, :] = meta.astype(BF16)


def padded(n):
    return (n + 7) // 8 * 8


def point_weights(meta, frame_ref, ox, oy, points):
    rows = padded(len(points))
    at = lax.broadcasted_iota(jnp.int32, (rows, K), 0)
    px = jnp.zeros((rows, K), F32)
    py = px
    for i, (a, b) in enumerate(points):
        px = jnp.where(at == i, center(a), px)
        py = jnp.where(at == i, center(b), py)
    rx = frame_ref[0].astype(F32)
    ry = frame_ref[1].astype(F32)
    x = meta[2:3] * (1.0 - 2.0 * rx) + (CT - 1.0) * rx
    y = meta[3:4] * (1.0 - 2.0 * ry) + (CT - 1.0) * ry
    dx = (x + float(ox * CT)) - px
    dy = (y + float(oy * CT)) - py
    sq = dx * dx + dy * dy
    inside = sq < float(RLOC * RLOC)
    out = []
    for rate in (2.0, 4.5):
        out.append(jnp.where(inside, jnp.exp(-sq * (rate / (RLOC * RLOC))), 0.0) * meta[1:2])
    return out


def add_up(points, rows, block, frame_ref, sw_ref, wp_ref, s_ref, put_gram, put_pull):
    seen = sorted({t for p in points for t in tiles_of(p, rows)})
    place = {t: i for i, t in enumerate(seen)}
    n = padded(len(points))
    for t in seen:
        meta = block(t)[K:ROWS, :].astype(F32)
        w = point_weights(meta, frame_ref, t[0], t[1], points)
        lanes = slice(place[t] * K, place[t] * K + K)
        for g in range(2):
            sw_ref[place[t], g * n : g * n + n, :] = jnp.sqrt(w[g])
        hi, lo = split(jnp.concatenate(w, 0) * meta[0:1])
        wp_ref[0 : 2 * n, lanes] = hi
        wp_ref[2 * n : 4 * n, lanes] = lo
    anom_seen = jnp.concatenate([block(t)[0:K, :] for t in seen], 1)
    pull = lax.dot_general(anom_seen, wp_ref[...], NT, preferred_element_type=F32)
    put_pull(pull[:, 0 : 2 * n] + pull[:, 2 * n : 4 * n])
    for i, p in enumerate(points):
        own = tiles_of(p, rows)
        for j, t in enumerate(own):
            anom = block(t)[0:K, :].astype(F32)
            for g in range(2):
                scale = sw_ref[place[t], g * n + i : g * n + i + 1, :]
                s_ref[i % 2, g, :, j * K : j * K + K] = (anom * scale).astype(BF16)
        for g in range(2):
            s = s_ref[i % 2, g, :, 0 : len(own) * K]
            put_gram(i, g, lax.dot_general(s, s, NT, preferred_element_type=F32))


def sum_scratch(points, rows):
    n = padded(len(points))
    seen = len({t for p in points for t in tiles_of(p, rows)})
    most = max(len(tiles_of(p, rows)) for p in points)
    return [
        pltpu.VMEM((seen, 2 * n, K), F32),
        pltpu.VMEM((4 * n, seen * K), BF16),
        pltpu.VMEM((2, 2, K, most * K), BF16),
    ]


def near_kernel(frame_ref, pair_ref, a_ref, b_ref, ta_ref, tb_ref, first_ref, rest_ref, pull_ref, *scratch):
    def block(t):
        ox, oy = t
        if ox <= 0:
            return (pair_ref, ta_ref, tb_ref)[-ox].at[oy if ox == 0 else 1 - oy]
        return (a_ref, b_ref)[ox - 1].at[oy]

    def put_gram(i, g, value):
        if i < FIRST:
            first_ref[2 * i + g] = value
        else:
            rest_ref[2 * (i - FIRST) + g] = value

    def put_pull(value):
        pull_ref[...] = value

    add_up(POINTS, (0, 1), block, frame_ref, *scratch, put_gram, put_pull)


def points_kernel(points, rows, batch, frame_ref, y_ref, z_ref, gram_ref, pull_in_ref, out_ref, sw, wp, s, g_ref, pull_ref):
    n = padded(len(points))
    skip = POINTS.index(points[0])

    def block(t):
        ox, oy = t
        if oy == -1:
            return y_ref.at[2 - ox]
        if oy == -2:
            return y_ref.at[6 - ox]
        return z_ref.at[2 + ox]

    def put_gram(i, g, value):
        g_ref[2 * i + g] = value

    def put_pull(value):
        pull_ref[...] = value

    add_up(points, rows, block, frame_ref, sw, wp, s, put_gram, put_pull)
    row = lax.broadcasted_iota(jnp.int32, (K, K), 0)
    col = lax.broadcasted_iota(jnp.int32, (K, K), 1)
    eye = jnp.where(row == col, 1.0, 0.0).astype(F32)
    total = 2 * len(points)
    for start in range(0, total, batch):
        ids = range(start, min(start + batch, total))
        xs, norms = [], []
        for i in ids:
            system = eye + (gram_ref[i] + g_ref[i]) * (1.0 / (K - 1.0))
            sq = jnp.sum(jnp.sum(system * system, 0, keepdims=True), 1, keepdims=True)
            norm = jnp.sqrt(sq)
            norms.append(norm)
            xs.append(system * (1.0 / norm))
        zs = four_steps(xs, eye)
        for i, z, norm in zip(ids, zs, norms):
            p, g = i // 2, i % 2
            near = g * len(POINTS) + skip + p
            far = g * n + p
            pull = pull_in_ref[:, near : near + 1] + pull_ref[:, far : far + 1]
            inner = jnp.sum(z * pull, 0, keepdims=True)
            shift = jnp.sum(z * inner, 1, keepdims=True) * (1.0 / (norm * (K - 1.0)))
            out_ref[p, g] = (z * (1.0 / jnp.sqrt(norm)) + shift).astype(BF16)


def specs(n):
    return [pl.BlockSpec(memory_space=pltpu.SMEM)] + [pl.BlockSpec(memory_space=pltpu.VMEM)] * n


def near_sums(frame, *blocks):
    n = len(POINTS)
    return pl.pallas_call(
        near_kernel,
        out_shape=[
            jax.ShapeDtypeStruct((2 * FIRST, K, K), F32),
            jax.ShapeDtypeStruct((2 * (n - FIRST), K, K), F32),
            jax.ShapeDtypeStruct((K, 2 * n), F32),
        ],
        in_specs=specs(len(blocks)),
        scratch_shapes=sum_scratch(POINTS, (0, 1)),
        compiler_params=pltpu.CompilerParams(vmem_limit_bytes=VMEM),
        cost_estimate=pl.CostEstimate(flops=6_000_000_000, bytes_accessed=5_000_000, transcendentals=0),
        name="near_sums",
    )(frame, *blocks)


def transforms(points, rows, batch, frame, y, z, gram, pull, name):
    n = len(points)
    return pl.pallas_call(
        functools.partial(points_kernel, points, rows, batch),
        out_shape=jax.ShapeDtypeStruct((n, 2, K, K), BF16),
        in_specs=specs(4),
        scratch_shapes=sum_scratch(points, rows)
        + [pltpu.VMEM((2 * n, K, K), F32), pltpu.VMEM((K, 2 * padded(n)), F32)],
        compiler_params=pltpu.CompilerParams(vmem_limit_bytes=VMEM),
        cost_estimate=pl.CostEstimate(flops=n * 700_000_000, bytes_accessed=4_000_000, transcendentals=0),
        name=name,
    )(frame, y, z, gram, pull)


def apply_kernel(frame_ref, ens_ref, first_ref, rest_ref, low_ref, high_ref, out_ref, rim_ref):
    side = APX + 2
    rx, ry = frame_ref[0], frame_ref[1]

    @pl.when(frame_ref[2] != 0)
    def _():
        for x in range(side):
            rim_ref[x] = first_ref[x]

    @pl.when(frame_ref[2] == 0)
    def _():
        for x in range(side):
            rim_ref[x] = low_ref[side - 1 - x]

    def transform(x, y, g):
        if y == 0:
            return rim_ref[x, g]
        if y == 1:
            return first_ref[x, g]
        if y == APX + 1:
            return high_ref[side - 1 - x, g]
        return rest_ref[(y - 2) * side + x, g]

    ones = jnp.ones((K, K), BF16)
    frac = [(s + 0.5) / SPACING for s in range(SPACING)]
    corner = [[1.0 - f for f in frac], frac]
    for q in range(APX + 1):
        for p in range(APX + 1):
            cells = [
                (s, t)
                for s in range(2)
                for t in range(2)
                if 0 <= 2 * q - 1 + s < CT and 0 <= 2 * p - 1 + t < CT
            ]
            at = []
            for s, t in cells:
                i, j = 2 * q - 1 + s, 2 * p - 1 + t
                at.append((i + rx * (CT - 1 - 2 * i), j + ry * (CT - 1 - 2 * j)))
            ens = jnp.concatenate([ens_ref[i, j] for i, j in at], 0)
            mean = lax.dot_general(ens, ones, NN, preferred_element_type=F32) * (1.0 / K)
            anom = (ens.astype(F32) - mean).astype(BF16)
            for g in range(2):
                spans = [
                    slice(c * 2 * NHALF + g * NHALF, c * 2 * NHALF + (g + 1) * NHALF)
                    for c in range(len(cells))
                ]
                left = jnp.concatenate([anom[sp] for sp in spans], 0)
                adds = [None] * len(cells)
                for cx in range(2):
                    for cy in range(2):
                        prod = lax.dot_general(
                            left, transform(q + cx, p + cy, g), NN, preferred_element_type=F32
                        )
                        for c, (s, t) in enumerate(cells):
                            term = prod[c * NHALF : (c + 1) * NHALF] * (corner[cx][s] * corner[cy][t])
                            adds[c] = term if adds[c] is None else adds[c] + term
                for c, (i, j) in enumerate(at):
                    out_ref[i, j, g * NHALF : (g + 1) * NHALF, :] = (mean[spans[c]] + adds[c]).astype(BF16)


def apply(frame, ensemble, first, rest, low, high):
    return pl.pallas_call(
        apply_kernel,
        out_shape=jax.ShapeDtypeStruct(ensemble.shape, BF16),
        in_specs=specs(5),
        scratch_shapes=[pltpu.VMEM((APX + 2, 2, K, K), BF16)],
        compiler_params=pltpu.CompilerParams(vmem_limit_bytes=VMEM),
        name="apply_transforms",
    )(frame, ensemble, first, rest, low, high)


def moved(block, source, sizes):
    nx, ny = sizes
    pairs = []
    for x in range(nx):
        for y in range(ny):
            at = source(x, y)
            if at is not None:
                pairs.append((at[0] % nx * ny + at[1], x * ny + y))
    return lax.ppermute(block, ("gx", "gy"), pairs)


def shards(ensemble, obs_anom, obs_innov, obs_prec, obs_pos, obs_count):
    sizes = (lax.axis_size("gx"), lax.axis_size("gy"))

    def core(x, y):
        return x, y ^ 1

    def side(distance):
        return lambda x, y: (x + distance * (1 - 2 * ((x ^ y) & 1)), y)

    def beyond(x, y):
        at = y + 2 * (y & 1) - 1
        return (x, at) if 0 <= at < sizes[1] else None

    own = pl.pallas_call(
        pack_kernel,
        out_shape=jax.ShapeDtypeStruct((ROWS, K), BF16),
        in_specs=specs(4),
        name="pack_slots",
    )(
        obs_count,
        obs_anom.reshape(K, K),
        obs_innov.reshape(1, K),
        obs_prec.reshape(1, K),
        obs_pos.reshape(2, K),
    )
    col, row = lax.axis_index("gx"), lax.axis_index("gy")
    ry = row & 1
    rx = (col ^ row) & 1
    edge = jnp.where((row == 0) | (row == sizes[1] - 1), 1, 0)
    frame = jnp.stack([rx, ry, edge]).astype(jnp.int32)

    pair = jnp.stack([own, moved(own, core, sizes)])
    a = moved(pair, side(1), sizes)
    b = moved(pair, side(2), sizes)
    ta = moved(a, core, sizes)
    tb = moved(b, core, sizes)
    wide = jnp.stack([tb[1], ta[1], pair[0], a[0], b[0], ta[0], pair[1], a[1]])
    y = moved(wide, beyond, sizes)
    gram_first, gram_rest, pull = near_sums(frame, pair, a, b, ta, tb)
    first = transforms(POINTS[:FIRST], (-2, -1), 12, frame, y, y, gram_first, pull, "first_points")
    low = moved(first, beyond, sizes)
    z = moved(y, core, sizes)
    rest = transforms(POINTS[FIRST:], (-2, -1, 2), 12, frame, y, z, gram_rest, pull, "rest_points")
    high = moved(rest[-FIRST:], core, sizes)
    return apply(frame, ensemble, first, rest, low, high)


def solution(mesh):
    placed = (
        P("gx", "gy", None, None),
        P("gx", "gy", None, None),
        P("gx", "gy", None),
        P("gx", "gy", None),
        P("gx", "gy", None, None),
        P("gx", "gy"),
    )
    return jax.shard_map(
        shards, mesh=mesh, in_specs=placed, out_specs=P("gx", "gy", None, None), check_vma=False
    )
```

```python
import functools

import jax
import jax.numpy as jnp
from jax import lax
from jax.experimental import pallas as pl
from jax.experimental.pallas import tpu as pltpu
from jax.sharding import PartitionSpec as P

K = 128
APX = 4
CT = 8
SPACING = 2
RLOC = 12
NHALF = 32
META = 4
ROWS = K + 16
PAIR = 2 * K + 16
WIDE = 10 * K + 48

NT = (((1,), (1,)), ((), ()))
NN = (((1,), (0,)), ((), ()))
F32 = jnp.float32
BF16 = jnp.bfloat16

SIDE = APX + 2
POINTS = [(a, b) for b in range(-1, APX) for a in range(-1, APX + 1)]
FIRST = 3 * SIDE


def center(a):
    return SPACING * a + (SPACING - 1) / 2.0


def least_distance(offset, point):
    return min(abs(offset * CT + s - center(point)) for s in range(CT))


def tiles_of(point, rows):
    a, b = point
    return [
        (ox, oy)
        for oy in rows
        for ox in range(-2, 3)
        if least_distance(ox, a) ** 2 + least_distance(oy, b) ** 2 < RLOC * RLOC
    ]


def split(x):
    hi = x.astype(BF16)
    lo = (x - hi.astype(F32)).astype(BF16)
    return hi, lo


def mm(a, b):
    left = jnp.concatenate([a[0], a[1]], 1)
    right = jnp.concatenate([b[0], b[1]], 1)
    right = jnp.concatenate([right, right], 0)
    out = lax.dot_general(left, right, NN, preferred_element_type=F32)
    return out[:, :K] + out[:, K:]


C0, C1, C2, C3, C4 = 2.25, -2.4375, 1.6875, -0.5625, 0.0625


def two_steps(xs, parts, eye):
    n = range(len(xs))
    sq = [mm(parts[i], parts[i]) for i in n]
    high = [mm(split(sq[i]), split(C3 * xs[i] + C4 * sq[i])) for i in n]
    return [C0 * eye + C1 * xs[i] + C2 * sq[i] + high[i] for i in n]


def four_steps(xs, eye):
    n = range(len(xs))
    x_parts = [split(x) for x in xs]
    z = two_steps(xs, x_parts, eye)
    z_parts = [split(v) for v in z]
    z_sq = [mm(z_parts[i], z_parts[i]) for i in n]
    m = [mm(x_parts[i], split(z_sq[i])) for i in n]
    q = two_steps(m, [split(v) for v in m], eye)
    return [mm(z_parts[i], split(q[i])) for i in n]


def pack_kernel(count_ref, anom_ref, innov_ref, prec_ref, pos_ref, out_ref):
    out_ref[0:K, :] = anom_ref[...].astype(F32).T.astype(BF16)
    slot = lax.broadcasted_iota(jnp.int32, (1, K), 1)
    live = jnp.where(slot < count_ref[0, 0], prec_ref[...].astype(F32), 0.0)
    meta = jnp.concatenate(
        [innov_ref[...].astype(F32), live, pos_ref[...].astype(F32), jnp.zeros((12, K), F32)], 0
    )
    out_ref[K:ROWS, :] = meta.astype(BF16)


def pair_kernel(own_ref, other_ref, out_ref):
    out_ref[0:K, :] = own_ref[0:K, :]
    out_ref[K : 2 * K, :] = other_ref[0:K, :]
    meta = [ref[K:ROWS, :].astype(F32)[0:META] for ref in (own_ref, other_ref)]
    out_ref[2 * K : PAIR, :] = jnp.concatenate(meta + [jnp.zeros((8, K), F32)], 0).astype(BF16)


def wide_kernel(pair_ref, a_ref, b_ref, ta_ref, tb_ref, out_ref):
    parts = [(tb_ref, 1), (ta_ref, 1), (pair_ref, 0), (a_ref, 0), (b_ref, 0)]
    parts += [(tb_ref, 0), (ta_ref, 0), (pair_ref, 1), (a_ref, 1), (b_ref, 1)]
    meta = []
    for k, (ref, row) in enumerate(parts):
        out_ref[k * K : k * K + K, :] = ref[row * K : row * K + K, :]
        meta.append(ref[2 * K : PAIR, :].astype(F32)[row * META : row * META + META])
    meta.append(jnp.zeros((8, K), F32))
    out_ref[10 * K : WIDE, :] = jnp.concatenate(meta, 0).astype(BF16)


def padded(n):
    return (n + 7) // 8 * 8


def point_weights(meta, frame_ref, ox, oy, points):
    rows = padded(len(points))
    at = lax.broadcasted_iota(jnp.int32, (rows, K), 0)
    px = jnp.zeros((rows, K), F32)
    py = px
    for i, (a, b) in enumerate(points):
        px = jnp.where(at == i, center(a), px)
        py = jnp.where(at == i, center(b), py)
    rx = frame_ref[0].astype(F32)
    ry = frame_ref[1].astype(F32)
    x = meta[2:3] * (1.0 - 2.0 * rx) + (CT - 1.0) * rx
    y = meta[3:4] * (1.0 - 2.0 * ry) + (CT - 1.0) * ry
    dx = (x + float(ox * CT)) - px
    dy = (y + float(oy * CT)) - py
    sq = dx * dx + dy * dy
    inside = sq < float(RLOC * RLOC)
    out = []
    for rate in (2.0, 4.5):
        out.append(jnp.where(inside, jnp.exp(-sq * (rate / (RLOC * RLOC))), 0.0) * meta[1:2])
    return out


def add_up(points, rows, block, frame_ref, sw_ref, wp_ref, s_ref, put_gram, put_pull):
    seen = sorted({t for p in points for t in tiles_of(p, rows)})
    place = {t: i for i, t in enumerate(seen)}
    n = padded(len(points))

    def anom(t):
        ref, k = block(t)
        return ref[k * K : k * K + K, :]

    metas = {}
    for t in seen:
        ref, k = block(t)
        if id(ref) not in metas:
            metas[id(ref)] = ref[10 * K : WIDE, :].astype(F32)
        meta = metas[id(ref)][k * META : k * META + META]
        w = point_weights(meta, frame_ref, t[0], t[1], points)
        lanes = slice(place[t] * K, place[t] * K + K)
        for g in range(2):
            sw_ref[place[t], g * n : g * n + n, :] = jnp.sqrt(w[g])
        hi, lo = split(jnp.concatenate(w, 0) * meta[0:1])
        wp_ref[0 : 2 * n, lanes] = hi
        wp_ref[2 * n : 4 * n, lanes] = lo
    anom_seen = jnp.concatenate([anom(t) for t in seen], 1)
    pull = lax.dot_general(anom_seen, wp_ref[...], NT, preferred_element_type=F32)
    put_pull(pull[:, 0 : 2 * n] + pull[:, 2 * n : 4 * n])
    for i, p in enumerate(points):
        own = tiles_of(p, rows)
        for j, t in enumerate(own):
            rows_in = anom(t).astype(F32)
            for g in range(2):
                scale = sw_ref[place[t], g * n + i : g * n + i + 1, :]
                s_ref[i % 2, g, :, j * K : j * K + K] = (rows_in * scale).astype(BF16)
        for g in range(2):
            s = s_ref[i % 2, g, :, 0 : len(own) * K]
            put_gram(i, g, lax.dot_general(s, s, NT, preferred_element_type=F32))


def sum_scratch(points, rows):
    n = padded(len(points))
    seen = len({t for p in points for t in tiles_of(p, rows)})
    most = max(len(tiles_of(p, rows)) for p in points)
    return [
        pltpu.VMEM((seen, 2 * n, K), F32),
        pltpu.VMEM((4 * n, seen * K), BF16),
        pltpu.VMEM((2, 2, K, most * K), BF16),
    ]


def near_kernel(frame_ref, wide_ref, first_ref, rest_ref, pull_ref, *scratch):
    def block(t):
        return wide_ref, 5 * t[1] + 2 + t[0]

    def put_gram(i, g, value):
        if i < FIRST:
            first_ref[2 * i + g] = value
        else:
            rest_ref[2 * (i - FIRST) + g] = value

    def put_pull(value):
        pull_ref[...] = value

    add_up(POINTS, (0, 1), block, frame_ref, *scratch, put_gram, put_pull)


def points_kernel(points, rows, batch, *refs):
    frame_ref, y_ref = refs[0:2]
    z_ref = refs[2] if 2 in rows else None
    gram_ref, pull_in_ref, out_ref, sw, wp, s, g_ref, pull_ref = refs[-8:]
    n = padded(len(points))
    skip = POINTS.index(points[0])

    def block(t):
        ox, oy = t
        if oy == 2:
            return z_ref, 2 + ox
        return y_ref, (2 if oy == -1 else 7) - ox

    def put_gram(i, g, value):
        g_ref[2 * i + g] = gram_ref[2 * i + g] + value

    def put_pull(value):
        pull_ref[...] = value

    add_up(points, rows, block, frame_ref, sw, wp, s, put_gram, put_pull)
    row = lax.broadcasted_iota(jnp.int32, (K, K), 0)
    col = lax.broadcasted_iota(jnp.int32, (K, K), 1)
    eye = jnp.where(row == col, 1.0, 0.0).astype(F32)
    total = 2 * len(points)
    for start in range(0, total, batch):
        ids = range(start, min(start + batch, total))
        xs, norms = [], []
        for i in ids:
            system = eye + g_ref[i] * (1.0 / (K - 1.0))
            sq = jnp.sum(jnp.sum(system * system, 0, keepdims=True), 1, keepdims=True)
            norm = jnp.sqrt(sq)
            norms.append(norm)
            xs.append(system * (1.0 / norm))
        zs = four_steps(xs, eye)
        for i, z, norm in zip(ids, zs, norms):
            p, g = i // 2, i % 2
            near = g * padded(len(POINTS)) + skip + p
            far = g * n + p
            pull = pull_in_ref[:, near : near + 1] + pull_ref[:, far : far + 1]
            inner = jnp.sum(z * pull, 0, keepdims=True)
            shift = jnp.sum(z * inner, 1, keepdims=True) * (1.0 / (norm * (K - 1.0)))
            out_ref[p, g] = (z * (1.0 / jnp.sqrt(norm)) + shift).astype(BF16)


def specs(n, scalars=1):
    return [pl.BlockSpec(memory_space=pltpu.SMEM)] * scalars + [pl.BlockSpec(memory_space=pltpu.VMEM)] * n


def joined(kernel, rows, name, *blocks):
    return pl.pallas_call(
        kernel,
        out_shape=jax.ShapeDtypeStruct((rows, K), BF16),
        in_specs=specs(len(blocks), 0),
        name=name,
    )(*blocks)


def near_sums(frame, wide):
    n = len(POINTS)
    return pl.pallas_call(
        near_kernel,
        out_shape=[
            jax.ShapeDtypeStruct((2 * FIRST, K, K), F32),
            jax.ShapeDtypeStruct((2 * (n - FIRST), K, K), F32),
            jax.ShapeDtypeStruct((K, 2 * padded(n)), F32),
        ],
        in_specs=specs(1),
        scratch_shapes=sum_scratch(POINTS, (0, 1)),
        compiler_params=pltpu.CompilerParams(vmem_limit_bytes=16 << 20),
        cost_estimate=pl.CostEstimate(flops=6_000_000_000, bytes_accessed=5_000_000, transcendentals=0),
        name="near_sums",
    )(frame, wide)


def transforms(points, rows, batch, name, frame, *arrays):
    n = len(points)
    return pl.pallas_call(
        functools.partial(points_kernel, points, rows, batch),
        out_shape=jax.ShapeDtypeStruct((n, 2, K, K), BF16),
        in_specs=specs(len(arrays)),
        scratch_shapes=sum_scratch(points, rows)
        + [pltpu.VMEM((2 * n, K, K), F32), pltpu.VMEM((K, 2 * padded(n)), F32)],
        compiler_params=pltpu.CompilerParams(vmem_limit_bytes=28 << 20),
        cost_estimate=pl.CostEstimate(flops=n * 500_000_000, bytes_accessed=4_000_000, transcendentals=0),
        name=name,
    )(frame, *arrays)


def anomalies_kernel(ens_ref, anom_ref, mean_ref):
    ones = jnp.ones((K, K), BF16)
    rows = CT * 2 * NHALF
    for i in range(CT):
        ens = ens_ref[i].reshape(rows, K)
        mean = lax.dot_general(ens, ones, NN, preferred_element_type=F32) * (1.0 / K)
        anom_ref[i] = (ens.astype(F32) - mean).astype(BF16).reshape(CT, 2 * NHALF, K)
        mean_ref[i] = mean.reshape(CT, 2 * NHALF, K)


def anomalies(ensemble):
    return pl.pallas_call(
        anomalies_kernel,
        out_shape=[
            jax.ShapeDtypeStruct(ensemble.shape, BF16),
            jax.ShapeDtypeStruct(ensemble.shape, F32),
        ],
        in_specs=specs(1, 0),
        compiler_params=pltpu.CompilerParams(vmem_limit_bytes=12 << 20),
        cost_estimate=pl.CostEstimate(flops=1_000_000_000, bytes_accessed=4_000_000, transcendentals=0),
        name="anomalies",
    )(ensemble)


def apply_kernel(frame_ref, anom_ref, mean_ref, first_ref, rest_ref, high_ref, out_ref):
    rx, ry, edge = frame_ref[0], frame_ref[1], frame_ref[2]

    def transform(x, y, g):
        if y == 0:
            return first_ref[x + edge * SIDE, g]
        if y < 3:
            return first_ref[y * SIDE + x, g]
        if y <= APX:
            return rest_ref[(y - 3) * SIDE + x, g]
        return high_ref[SIDE - 1 - x, g]

    frac = [(s + 0.5) / SPACING for s in range(SPACING)]
    corner = [[1.0 - f for f in frac], frac]
    for p in range(APX + 1):
        for q in range(APX + 1):
            cells = []
            for s in range(2):
                for t in range(2):
                    i, j = 2 * q - 1 + s, 2 * p - 1 + t
                    if 0 <= i < CT and 0 <= j < CT:
                        cells.append((s, t, i + rx * (CT - 1 - 2 * i), j + ry * (CT - 1 - 2 * j)))
            for g in range(2):
                span = slice(g * NHALF, (g + 1) * NHALF)
                left = jnp.concatenate([anom_ref[i, j, span, :] for _, _, i, j in cells], 0)
                sums = [mean_ref[i, j, span, :] for _, _, i, j in cells]
                for cx in range(2):
                    both = jnp.concatenate([transform(q + cx, p + cy, g) for cy in range(2)], 1)
                    prod = lax.dot_general(left, both, NN, preferred_element_type=F32)
                    for cy in range(2):
                        for c, (s, t, _, _) in enumerate(cells):
                            part = prod[c * NHALF : (c + 1) * NHALF, cy * K : (cy + 1) * K]
                            sums[c] = sums[c] + part * (corner[cx][s] * corner[cy][t])
                for total, (_, _, i, j) in zip(sums, cells):
                    out_ref[i, j, span, :] = total.astype(BF16)


def apply(frame, anom, mean, first, rest, high):
    return pl.pallas_call(
        apply_kernel,
        out_shape=jax.ShapeDtypeStruct(anom.shape, BF16),
        in_specs=specs(5),
        compiler_params=pltpu.CompilerParams(vmem_limit_bytes=16 << 20),
        name="apply_transforms",
    )(frame, anom, mean, first, rest, high)


def moved(block, source, sizes):
    nx, ny = sizes
    pairs = []
    for x in range(nx):
        for y in range(ny):
            at = source(x, y)
            if at is not None:
                pairs.append((at[0] % nx * ny + at[1], x * ny + y))
    return lax.ppermute(block, ("gx", "gy"), pairs)


def shards(ensemble, obs_anom, obs_innov, obs_prec, obs_pos, obs_count):
    sizes = (lax.axis_size("gx"), lax.axis_size("gy"))

    def core(x, y):
        return x, y ^ 1

    def side(distance):
        return lambda x, y: (x + distance * (1 - 2 * ((x ^ y) & 1)), y)

    def beyond(x, y):
        at = y + 2 * (y & 1) - 1
        return (x, at) if 0 <= at < sizes[1] else None

    own = pl.pallas_call(
        pack_kernel,
        out_shape=jax.ShapeDtypeStruct((ROWS, K), BF16),
        in_specs=specs(4),
        name="pack_slots",
    )(
        obs_count,
        obs_anom.reshape(K, K),
        obs_innov.reshape(1, K),
        obs_prec.reshape(1, K),
        obs_pos.reshape(2, K),
    )
    col, row = lax.axis_index("gx"), lax.axis_index("gy")
    edge = jnp.where((row == 0) | (row == sizes[1] - 1), 1, 0)
    frame = jnp.stack([(col ^ row) & 1, row & 1, edge]).astype(jnp.int32)

    pair = joined(pair_kernel, PAIR, "pair_tiles", own, moved(own, core, sizes))
    a = moved(pair, side(1), sizes)
    b = moved(pair, side(2), sizes)
    ta = moved(a, core, sizes)
    tb = moved(b, core, sizes)
    wide = joined(wide_kernel, WIDE, "two_rows", pair, a, b, ta, tb)
    y = moved(wide, beyond, sizes)
    anom, mean = anomalies(ensemble)
    gram_first, gram_rest, pull = near_sums(frame, wide)
    y, pull = lax.optimization_barrier((y, pull))
    z = moved(y, core, sizes)
    first = transforms(POINTS[:FIRST], (-2, -1), 12, "first_points", frame, y, gram_first, pull)
    rest = transforms(POINTS[FIRST:], (-1, 2), 12, "rest_points", frame, y, z, gram_rest, pull)
    high = moved(rest[-SIDE:], core, sizes)
    return apply(frame, anom, mean, first, rest, high)


def solution(mesh):
    placed = (
        P("gx", "gy", None, None),
        P("gx", "gy", None, None),
        P("gx", "gy", None),
        P("gx", "gy", None),
        P("gx", "gy", None, None),
        P("gx", "gy"),
    )
    return jax.shard_map(
        shards, mesh=mesh, in_specs=placed, out_specs=P("gx", "gy", None, None), check_vma=False
    )
```

```python
import functools

import jax
import jax.numpy as jnp
from jax import lax
from jax.experimental import pallas as pl
from jax.experimental.pallas import tpu as pltpu
from jax.sharding import PartitionSpec as P

K = 128
APX = 4
CT = 8
SPACING = 2
RLOC = 12
NHALF = 32
META = 4
ROWS = K + 16
PAIR = 2 * K + 16
WIDE = 5 * K + 32
SLOTS = 2
LAG = 10

NT = (((1,), (1,)), ((), ()))
NN = (((1,), (0,)), ((), ()))
F32 = jnp.float32
BF16 = jnp.bfloat16

SIDE = APX + 2
POINTS = [(a, b) for b in range(-1, APX) for a in range(-1, APX + 1)]
FIRST = 3 * SIDE


def center(a):
    return SPACING * a + (SPACING - 1) / 2.0


def least_distance(offset, point):
    return min(abs(offset * CT + s - center(point)) for s in range(CT))


def tiles_of(point, rows):
    a, b = point
    return [
        (ox, oy)
        for oy in rows
        for ox in range(-2, 3)
        if least_distance(ox, a) ** 2 + least_distance(oy, b) ** 2 < RLOC * RLOC
    ]


def split(x):
    hi = x.astype(BF16)
    lo = (x - hi.astype(F32)).astype(BF16)
    return hi, lo


def mm(a, b):
    left = jnp.concatenate([a[0], a[1]], 1)
    right = jnp.concatenate([b[0], b[1]], 1)
    right = jnp.concatenate([right, right], 0)
    out = lax.dot_general(left, right, NN, preferred_element_type=F32)
    return out[:, :K] + out[:, K:]


def rounded(x):
    return (x.astype(BF16),)


def mm_high(a, b):
    return lax.dot_general(a[0], b[0], NN, preferred_element_type=F32)


C0, C1, C2, C3, C4 = 2.25, -2.4375, 1.6875, -0.5625, 0.0625


def pack_kernel(count_ref, anom_ref, innov_ref, prec_ref, pos_ref, out_ref):
    out_ref[0:K, :] = anom_ref[...].astype(F32).T.astype(BF16)
    slot = lax.broadcasted_iota(jnp.int32, (1, K), 1)
    live = jnp.where(slot < count_ref[0, 0], prec_ref[...].astype(F32), 0.0)
    meta = jnp.concatenate(
        [innov_ref[...].astype(F32), live, pos_ref[...].astype(F32), jnp.zeros((12, K), F32)], 0
    )
    out_ref[K:ROWS, :] = meta.astype(BF16)


def pair_kernel(own_ref, other_ref, out_ref):
    out_ref[0:K, :] = own_ref[0:K, :]
    out_ref[K : 2 * K, :] = other_ref[0:K, :]
    meta = [ref[K:ROWS, :].astype(F32)[0:META] for ref in (own_ref, other_ref)]
    out_ref[2 * K : PAIR, :] = jnp.concatenate(meta + [jnp.zeros((8, K), F32)], 0).astype(BF16)


def rows_kernel(pair_ref, a_ref, b_ref, ta_ref, tb_ref, *out_refs):
    for row, out_ref in enumerate(out_refs):
        parts = [(tb_ref, 1 - row), (ta_ref, 1 - row), (pair_ref, row), (a_ref, row), (b_ref, row)]
        meta = []
        for k, (ref, at) in enumerate(parts):
            out_ref[k * K : k * K + K, :] = ref[at * K : at * K + K, :]
            meta.append(ref[2 * K : PAIR, :].astype(F32)[at * META : at * META + META])
        meta.append(jnp.zeros((12, K), F32))
        out_ref[5 * K : WIDE, :] = jnp.concatenate(meta, 0).astype(BF16)


def padded(n):
    return (n + 7) // 8 * 8


def point_weights(meta, frame_ref, ox, oy, points):
    rows = padded(len(points))
    at = lax.broadcasted_iota(jnp.int32, (rows, K), 0)
    px = jnp.zeros((rows, K), F32)
    py = px
    for i, (a, b) in enumerate(points):
        px = jnp.where(at == i, center(a), px)
        py = jnp.where(at == i, center(b), py)
    rx = frame_ref[0].astype(F32)
    ry = frame_ref[1].astype(F32)
    x = meta[2:3] * (1.0 - 2.0 * rx) + (CT - 1.0) * rx
    y = meta[3:4] * (1.0 - 2.0 * ry) + (CT - 1.0) * ry
    dx = (x + float(ox * CT)) - px
    dy = (y + float(oy * CT)) - py
    sq = dx * dx + dy * dy
    inside = sq < float(RLOC * RLOC)
    out = []
    for rate in (2.0, 4.5):
        out.append(jnp.where(inside, jnp.exp(-sq * (rate / (RLOC * RLOC))), 0.0) * meta[1:2])
    return out


def add_up(points, rows, block, frame_ref, sw_ref, wp_ref, s_ref, put_gram, put_pull):
    seen = sorted({t for p in points for t in tiles_of(p, rows)})
    place = {t: i for i, t in enumerate(seen)}
    n = padded(len(points))

    def anom(t):
        ref, k = block(t)
        return ref[k * K : k * K + K, :]

    metas = {}
    for t in seen:
        ref, k = block(t)
        if id(ref) not in metas:
            metas[id(ref)] = ref[5 * K : WIDE, :].astype(F32)
        meta = metas[id(ref)][k * META : k * META + META]
        w = point_weights(meta, frame_ref, t[0], t[1], points)
        lanes = slice(place[t] * K, place[t] * K + K)
        for g in range(2):
            sw_ref[place[t], g * n : g * n + n, :] = jnp.sqrt(w[g])
        hi, lo = split(jnp.concatenate(w, 0) * meta[0:1])
        wp_ref[0 : 2 * n, lanes] = hi
        wp_ref[2 * n : 4 * n, lanes] = lo
    anom_seen = jnp.concatenate([anom(t) for t in seen], 1)
    pull = lax.dot_general(wp_ref[...], anom_seen, NT, preferred_element_type=F32)
    put_pull(pull[0 : 2 * n] + pull[2 * n : 4 * n])

    def add_point(i):
        own = tiles_of(points[i], rows)
        for j, t in enumerate(own):
            rows_in = anom(t).astype(F32)
            for g in range(2):
                scale = sw_ref[place[t], g * n + i : g * n + i + 1, :]
                s_ref[i % SLOTS, g, :, j * K : j * K + K] = (rows_in * scale).astype(BF16)
        for g in range(2):
            s = s_ref[i % SLOTS, g, :, 0 : len(own) * K]
            put_gram(i, g, lax.dot_general(s, s, NT, preferred_element_type=F32))

    return add_point


def sum_scratch(points, rows):
    n = padded(len(points))
    seen = len({t for p in points for t in tiles_of(p, rows)})
    most = max(len(tiles_of(p, rows)) for p in points)
    return [
        pltpu.VMEM((seen, 2 * n, K), F32),
        pltpu.VMEM((4 * n, seen * K), BF16),
        pltpu.VMEM((SLOTS, 2, K, most * K), BF16),
    ]


def near_kernel(frame_ref, own_ref, other_ref, first_ref, rest_ref, pull_ref, *scratch):
    def block(t):
        return (own_ref, other_ref)[t[1]], 2 + t[0]

    def put_gram(i, g, value):
        if i < FIRST:
            first_ref[2 * i + g] = value
        else:
            rest_ref[2 * (i - FIRST) + g] = value

    def put_pull(value):
        pull_ref[...] = value

    add_point = add_up(POINTS, (0, 1), block, frame_ref, *scratch, put_gram, put_pull)
    for i in range(len(POINTS)):
        add_point(i)


def points_kernel(points, rows, batch, *refs):
    frame_ref = refs[0]
    row_refs = dict(zip(rows, refs[1:]))
    gram_ref, pull_in_ref, out_ref, sw, wp, s, g_ref, pull_ref = refs[-8:]
    n = padded(len(points))
    skip = POINTS.index(points[0])

    def block(t):
        ox, oy = t
        return row_refs[oy], 2 + (ox if oy == 2 else -ox)

    def put_gram(i, g, value):
        g_ref[2 * i + g] = gram_ref[2 * i + g] + value

    def put_pull(value):
        pull_ref[...] = value

    add_point = add_up(points, rows, block, frame_ref, sw, wp, s, put_gram, put_pull)
    row = lax.broadcasted_iota(jnp.int32, (K, K), 0)
    col = lax.broadcasted_iota(jnp.int32, (K, K), 1)
    eye = jnp.where(row == col, 1.0, 0.0).astype(F32)

    def steps(first):
        ids = [(p, g) for p in range(first, min(first + batch, len(points))) for g in range(2)]
        now = {}

        def gram():
            for p, g in ids[::2]:
                add_point(p)

        def scale():
            now["x"], now["norm"] = [], []
            for p, g in ids:
                system = eye + g_ref[2 * p + g] * (1.0 / (K - 1.0))
                sq = jnp.sum(jnp.sum(system * system, 0, keepdims=True), 1, keepdims=True)
                norm = jnp.sqrt(sq)
                now["norm"].append(norm)
                now["x"].append(system * (1.0 / norm))
            now["xs"] = [split(x) for x in now["x"]]

        def square(parts, out, times):
            def run():
                now[out] = [times(v, v) for v in now[parts]]

            return run

        def polynomial(x, sq, out, parts, times):
            def run():
                high = [times(parts(q), parts(C3 * v + C4 * q)) for v, q in zip(now[x], now[sq])]
                now[out] = [
                    split(C0 * eye + C1 * v + C2 * q + h) for v, q, h in zip(now[x], now[sq], high)
                ]

            return run

        def second():
            now["m"] = [mm(a, split(b)) for a, b in zip(now["xs"], now["w"])]
            now["ms"] = [split(v) for v in now["m"]]

        def inverse():
            now["i"] = [mm(a, b) for a, b in zip(now["z"], now["q"])]

        def write():
            for (p, g), z, norm in zip(ids, now["i"], now["norm"]):
                near = g * padded(len(POINTS)) + skip + p
                far = g * n + p
                pull = pull_in_ref[near : near + 1, :] + pull_ref[far : far + 1, :]
                inner = jnp.sum(z * pull, 1, keepdims=True)
                shift = jnp.sum(z * inner, 0, keepdims=True) * (1.0 / (norm * (K - 1.0)))
                out_ref[p, g] = (z * (1.0 / jnp.sqrt(norm)) + shift).astype(BF16)

        return [
            gram,
            scale,
            square("xs", "b", mm_high),
            polynomial("x", "b", "z", rounded, mm_high),
            square("z", "w", mm),
            second,
            square("ms", "c", mm),
            polynomial("m", "c", "q", split, mm),
            inverse,
            write,
        ]

    order = []
    for k, first in enumerate(range(0, len(points), batch)):
        order += [(k * LAG + j, k, step) for j, step in enumerate(steps(first))]
    for _, _, step in sorted(order, key=lambda e: e[:2]):
        step()


def specs(n, scalars=1):
    return [pl.BlockSpec(memory_space=pltpu.SMEM)] * scalars + [pl.BlockSpec(memory_space=pltpu.VMEM)] * n


def joined(kernel, rows, name, *blocks):
    return pl.pallas_call(
        kernel,
        out_shape=[jax.ShapeDtypeStruct((n, K), BF16) for n in rows],
        in_specs=specs(len(blocks), 0),
        compiler_params=pltpu.CompilerParams(vmem_limit_bytes=2 << 20),
        name=name,
    )(*blocks)


def near_sums(frame, own, other):
    n = len(POINTS)
    return pl.pallas_call(
        near_kernel,
        out_shape=[
            jax.ShapeDtypeStruct((2 * FIRST, K, K), F32),
            jax.ShapeDtypeStruct((2 * (n - FIRST), K, K), F32),
            jax.ShapeDtypeStruct((2 * padded(n), K), F32),
        ],
        in_specs=specs(2),
        scratch_shapes=sum_scratch(POINTS, (0, 1)),
        compiler_params=pltpu.CompilerParams(vmem_limit_bytes=16 << 20),
        cost_estimate=pl.CostEstimate(flops=6_000_000_000, bytes_accessed=5_000_000, transcendentals=0),
        name="near_sums",
    )(frame, own, other)


def transforms(points, rows, batch, name, frame, *arrays):
    n = len(points)
    return pl.pallas_call(
        functools.partial(points_kernel, points, rows, batch),
        out_shape=jax.ShapeDtypeStruct((n, 2, K, K), BF16),
        in_specs=specs(len(arrays)),
        scratch_shapes=sum_scratch(points, rows)
        + [pltpu.VMEM((2 * n, K, K), F32), pltpu.VMEM((2 * padded(n), K), F32)],
        compiler_params=pltpu.CompilerParams(vmem_limit_bytes=28 << 20),
        cost_estimate=pl.CostEstimate(flops=n * 500_000_000, bytes_accessed=4_000_000, transcendentals=0),
        name=name,
    )(frame, *arrays)


def anomalies_kernel(ens_ref, anom_ref, mean_ref):
    ones = jnp.ones((K, K), BF16)
    rows = CT * 2 * NHALF
    for i in range(CT):
        ens = ens_ref[i].reshape(rows, K)
        mean = lax.dot_general(ens, ones, NN, preferred_element_type=F32) * (1.0 / K)
        anom_ref[i] = (ens.astype(F32) - mean).astype(BF16).reshape(CT, 2 * NHALF, K)
        mean_ref[i] = mean.reshape(CT, 2 * NHALF, K)


def anomalies(ensemble):
    return pl.pallas_call(
        anomalies_kernel,
        out_shape=[
            jax.ShapeDtypeStruct(ensemble.shape, BF16),
            jax.ShapeDtypeStruct(ensemble.shape, F32),
        ],
        in_specs=specs(1, 0),
        compiler_params=pltpu.CompilerParams(vmem_limit_bytes=12 << 20),
        cost_estimate=pl.CostEstimate(flops=1_000_000_000, bytes_accessed=4_000_000, transcendentals=0),
        name="anomalies",
    )(ensemble)


def apply_kernel(frame_ref, anom_ref, mean_ref, first_ref, rest_ref, high_ref, out_ref):
    rx, ry, edge = frame_ref[0], frame_ref[1], frame_ref[2]

    def transform(x, y, g):
        if y == 0:
            return first_ref[x + edge * SIDE, g]
        if y < 3:
            return first_ref[y * SIDE + x, g]
        if y <= APX:
            return rest_ref[(y - 3) * SIDE + x, g]
        return high_ref[SIDE - 1 - x, g]

    frac = [(s + 0.5) / SPACING for s in range(SPACING)]
    corner = [[1.0 - f for f in frac], frac]
    for p in range(APX + 1):
        for q in range(APX + 1):
            cells = []
            for s in range(2):
                for t in range(2):
                    i, j = 2 * q - 1 + s, 2 * p - 1 + t
                    if 0 <= i < CT and 0 <= j < CT:
                        cells.append((s, t, i + rx * (CT - 1 - 2 * i), j + ry * (CT - 1 - 2 * j)))
            for g in range(2):
                span = slice(g * NHALF, (g + 1) * NHALF)
                left = jnp.concatenate([anom_ref[i, j, span, :] for _, _, i, j in cells], 0)
                sums = [mean_ref[i, j, span, :] for _, _, i, j in cells]
                for cx in range(2):
                    both = jnp.concatenate([transform(q + cx, p + cy, g) for cy in range(2)], 0)
                    prod = lax.dot_general(left, both, NT, preferred_element_type=F32)
                    for cy in range(2):
                        for c, (s, t, _, _) in enumerate(cells):
                            part = prod[c * NHALF : (c + 1) * NHALF, cy * K : (cy + 1) * K]
                            sums[c] = sums[c] + part * (corner[cx][s] * corner[cy][t])
                for total, (_, _, i, j) in zip(sums, cells):
                    out_ref[i, j, span, :] = total.astype(BF16)


def apply(frame, anom, mean, first, rest, high):
    return pl.pallas_call(
        apply_kernel,
        out_shape=jax.ShapeDtypeStruct(anom.shape, BF16),
        in_specs=specs(5),
        compiler_params=pltpu.CompilerParams(vmem_limit_bytes=16 << 20),
        name="apply_transforms",
    )(frame, anom, mean, first, rest, high)


def moved(block, source, sizes):
    nx, ny = sizes
    pairs = []
    for x in range(nx):
        for y in range(ny):
            at = source(x, y)
            if at is not None:
                pairs.append((at[0] % nx * ny + at[1], x * ny + y))
    return lax.ppermute(block, ("gx", "gy"), pairs)


def shards(ensemble, obs_anom, obs_innov, obs_prec, obs_pos, obs_count):
    sizes = (lax.axis_size("gx"), lax.axis_size("gy"))

    def core(x, y):
        return x, y ^ 1

    def side(distance):
        return lambda x, y: (x + distance * (1 - 2 * ((x ^ y) & 1)), y)

    def beyond(x, y):
        at = y + 2 * (y & 1) - 1
        return (x, at) if 0 <= at < sizes[1] else None

    own = pl.pallas_call(
        pack_kernel,
        out_shape=jax.ShapeDtypeStruct((ROWS, K), BF16),
        in_specs=specs(4),
        compiler_params=pltpu.CompilerParams(vmem_limit_bytes=2 << 20),
        name="pack_slots",
    )(
        obs_count,
        obs_anom.reshape(K, K),
        obs_innov.reshape(1, K),
        obs_prec.reshape(1, K),
        obs_pos.reshape(2, K),
    )
    col, row = lax.axis_index("gx"), lax.axis_index("gy")
    edge = jnp.where((row == 0) | (row == sizes[1] - 1), 1, 0)
    frame = jnp.stack([(col ^ row) & 1, row & 1, edge]).astype(jnp.int32)

    (pair,) = joined(pair_kernel, [PAIR], "pair_tiles", own, moved(own, core, sizes))
    a = moved(pair, side(1), sizes)
    b = moved(pair, side(2), sizes)
    ta = moved(a, core, sizes)
    tb = moved(b, core, sizes)
    near, next_row = joined(rows_kernel, [WIDE, WIDE], "two_rows", pair, a, b, ta, tb)
    y1 = moved(near, beyond, sizes)
    anom, mean = anomalies(ensemble)
    gram_first, gram_rest, pull = near_sums(frame, near, next_row)
    y2 = moved(lax.optimization_barrier((next_row, pull))[0], beyond, sizes)
    z = moved(lax.optimization_barrier((y1, pull))[0], core, sizes)
    rest = transforms(POINTS[FIRST:], (-1, 2), 12, "rest_points", frame, y1, z, gram_rest, pull)
    first = transforms(POINTS[:FIRST], (-2, -1), 9, "first_points", frame, y2, y1, gram_first, pull)
    high = moved(rest[-SIDE:], core, sizes)
    return apply(frame, anom, mean, first, rest, high)


def solution(mesh):
    placed = (
        P("gx", "gy", None, None),
        P("gx", "gy", None, None),
        P("gx", "gy", None),
        P("gx", "gy", None),
        P("gx", "gy", None, None),
        P("gx", "gy"),
    )
    return jax.shard_map(
        shards, mesh=mesh, in_specs=placed, out_specs=P("gx", "gy", None, None), check_vma=False
    )
```

```python
import functools

import jax
import jax.numpy as jnp
from jax import lax
from jax.experimental import pallas as pl
from jax.experimental.pallas import tpu as pltpu
from jax.sharding import PartitionSpec as P

K = 128
APX = 4
CT = 8
SPACING = 2
RLOC = 12
NHALF = 32
META = 4
ROWS = K + 16
PAIR = 2 * K + 16
WIDE = 5 * K + 32
SLOTS = 2
FLOPS = 500_000_000
LAG = 10

NT = (((1,), (1,)), ((), ()))
NN = (((1,), (0,)), ((), ()))
F32 = jnp.float32
BF16 = jnp.bfloat16

SIDE = APX + 2
POINTS = [(a, b) for b in range(-1, APX) for a in range(-1, APX + 1)]
FIRST = 3 * SIDE


def center(a):
    return SPACING * a + (SPACING - 1) / 2.0


def least_distance(offset, point):
    return min(abs(offset * CT + s - center(point)) for s in range(CT))


def tiles_of(point, rows):
    a, b = point
    return [
        (ox, oy)
        for oy in rows
        for ox in range(-2, 3)
        if least_distance(ox, a) ** 2 + least_distance(oy, b) ** 2 < RLOC * RLOC
    ]


def split(x):
    hi = x.astype(BF16)
    lo = (x - hi.astype(F32)).astype(BF16)
    return hi, lo


def mm(a, b):
    left = jnp.concatenate([a[0], a[1]], 1)
    right = jnp.concatenate([b[0], b[1]], 1)
    right = jnp.concatenate([right, right], 0)
    out = lax.dot_general(left, right, NN, preferred_element_type=F32)
    return out[:, :K] + out[:, K:]


def rounded(x):
    return (x.astype(BF16),)


def mm_high(a, b):
    return lax.dot_general(a[0], b[0], NN, preferred_element_type=F32)


C0, C1, C2, C3, C4 = 2.25, -2.4375, 1.6875, -0.5625, 0.0625


def pack_kernel(count_ref, anom_ref, innov_ref, prec_ref, pos_ref, out_ref):
    out_ref[0:K, :] = anom_ref[...].astype(F32).T.astype(BF16)
    slot = lax.broadcasted_iota(jnp.int32, (1, K), 1)
    live = jnp.where(slot < count_ref[0, 0], prec_ref[...].astype(F32), 0.0)
    meta = jnp.concatenate(
        [innov_ref[...].astype(F32), live, pos_ref[...].astype(F32), jnp.zeros((12, K), F32)], 0
    )
    out_ref[K:ROWS, :] = meta.astype(BF16)


def pair_kernel(own_ref, other_ref, out_ref):
    out_ref[0:K, :] = own_ref[0:K, :]
    out_ref[K : 2 * K, :] = other_ref[0:K, :]
    meta = [ref[K:ROWS, :].astype(F32)[0:META] for ref in (own_ref, other_ref)]
    out_ref[2 * K : PAIR, :] = jnp.concatenate(meta + [jnp.zeros((8, K), F32)], 0).astype(BF16)


def rows_kernel(pair_ref, a_ref, b_ref, ta_ref, tb_ref, *out_refs):
    for row, out_ref in enumerate(out_refs):
        parts = [(tb_ref, 1 - row), (ta_ref, 1 - row), (pair_ref, row), (a_ref, row), (b_ref, row)]
        meta = []
        for k, (ref, at) in enumerate(parts):
            out_ref[k * K : k * K + K, :] = ref[at * K : at * K + K, :]
            meta.append(ref[2 * K : PAIR, :].astype(F32)[at * META : at * META + META])
        meta.append(jnp.zeros((12, K), F32))
        out_ref[5 * K : WIDE, :] = jnp.concatenate(meta, 0).astype(BF16)


def padded(n):
    return (n + 7) // 8 * 8


def point_weights(meta, frame_ref, ox, oy, points):
    rows = padded(len(points))
    at = lax.broadcasted_iota(jnp.int32, (rows, K), 0)
    px = jnp.zeros((rows, K), F32)
    py = px
    for i, (a, b) in enumerate(points):
        px = jnp.where(at == i, center(a), px)
        py = jnp.where(at == i, center(b), py)
    rx = frame_ref[0].astype(F32)
    ry = frame_ref[1].astype(F32)
    x = meta[2:3] * (1.0 - 2.0 * rx) + (CT - 1.0) * rx
    y = meta[3:4] * (1.0 - 2.0 * ry) + (CT - 1.0) * ry
    dx = (x + float(ox * CT)) - px
    dy = (y + float(oy * CT)) - py
    sq = dx * dx + dy * dy
    inside = sq < float(RLOC * RLOC)
    out = []
    for rate in (2.0, 4.5):
        out.append(jnp.where(inside, jnp.exp(-sq * (rate / (RLOC * RLOC))), 0.0) * meta[1:2])
    return out


def add_up(points, rows, block, frame_ref, sw_ref, wp_ref, s_ref, put_gram, put_pull):
    seen = sorted({t for p in points for t in tiles_of(p, rows)})
    place = {t: i for i, t in enumerate(seen)}
    n = padded(len(points))

    def anom(t):
        ref, k = block(t)
        return ref[k * K : k * K + K, :]

    metas = {}
    for t in seen:
        ref, k = block(t)
        if id(ref) not in metas:
            metas[id(ref)] = ref[5 * K : WIDE, :].astype(F32)
        meta = metas[id(ref)][k * META : k * META + META]
        w = point_weights(meta, frame_ref, t[0], t[1], points)
        lanes = slice(place[t] * K, place[t] * K + K)
        for g in range(2):
            sw_ref[place[t], g * n : g * n + n, :] = jnp.sqrt(w[g])
        hi, lo = split(jnp.concatenate(w, 0) * meta[0:1])
        wp_ref[0 : 2 * n, lanes] = hi
        wp_ref[2 * n : 4 * n, lanes] = lo
    anom_seen = jnp.concatenate([anom(t) for t in seen], 1)
    pull = lax.dot_general(wp_ref[...], anom_seen, NT, preferred_element_type=F32)
    put_pull(pull[0 : 2 * n] + pull[2 * n : 4 * n])

    def add_point(i):
        own = tiles_of(points[i], rows)
        for j, t in enumerate(own):
            rows_in = anom(t).astype(F32)
            for g in range(2):
                scale = sw_ref[place[t], g * n + i : g * n + i + 1, :]
                s_ref[i % SLOTS, g, :, j * K : j * K + K] = (rows_in * scale).astype(BF16)
        for g in range(2):
            s = s_ref[i % SLOTS, g, :, 0 : len(own) * K]
            put_gram(i, g, lax.dot_general(s, s, NT, preferred_element_type=F32))

    return add_point


def sum_scratch(points, rows):
    n = padded(len(points))
    seen = len({t for p in points for t in tiles_of(p, rows)})
    most = max(len(tiles_of(p, rows)) for p in points)
    return [
        pltpu.VMEM((seen, 2 * n, K), F32),
        pltpu.VMEM((4 * n, seen * K), BF16),
        pltpu.VMEM((SLOTS, 2, K, most * K), BF16),
    ]


def near_kernel(frame_ref, own_ref, other_ref, first_ref, rest_ref, pull_ref, *scratch):
    def block(t):
        return (own_ref, other_ref)[t[1]], 2 + t[0]

    def put_gram(i, g, value):
        if i < FIRST:
            first_ref[2 * i + g] = value
        else:
            rest_ref[2 * (i - FIRST) + g] = value

    def put_pull(value):
        pull_ref[...] = value

    add_point = add_up(POINTS, (0, 1), block, frame_ref, *scratch, put_gram, put_pull)
    for i in range(len(POINTS)):
        add_point(i)


def points_kernel(points, rows, batch, *refs):
    frame_ref = refs[0]
    row_refs = dict(zip(rows, refs[1:]))
    gram_ref, pull_in_ref, out_ref, sw, wp, s, g_ref, pull_ref = refs[-8:]
    n = padded(len(points))
    skip = POINTS.index(points[0])

    def block(t):
        ox, oy = t
        return row_refs[oy], 2 + (ox if oy == 2 else -ox)

    def put_gram(i, g, value):
        g_ref[2 * i + g] = gram_ref[2 * i + g] + value

    def put_pull(value):
        pull_ref[...] = value

    add_point = add_up(points, rows, block, frame_ref, sw, wp, s, put_gram, put_pull)
    row = lax.broadcasted_iota(jnp.int32, (K, K), 0)
    col = lax.broadcasted_iota(jnp.int32, (K, K), 1)
    eye = jnp.where(row == col, 1.0, 0.0).astype(F32)

    def steps(first):
        ids = [(p, g) for p in range(first, min(first + batch, len(points))) for g in range(2)]
        now = {}

        def gram():
            for p, g in ids[::2]:
                add_point(p)

        def scale():
            now["x"], now["norm"] = [], []
            for p, g in ids:
                system = eye + g_ref[2 * p + g] * (1.0 / (K - 1.0))
                sq = jnp.sum(jnp.sum(system * system, 0, keepdims=True), 1, keepdims=True)
                norm = jnp.sqrt(sq)
                now["norm"].append(norm)
                now["x"].append(system * (1.0 / norm))
            now["xs"] = [split(x) for x in now["x"]]

        def square(parts, out, times):
            def run():
                now[out] = [times(v, v) for v in now[parts]]

            return run

        def polynomial(x, sq, out, parts, times):
            def run():
                high = [times(parts(q), parts(C3 * v + C4 * q)) for v, q in zip(now[x], now[sq])]
                now[out] = [
                    split(C0 * eye + C1 * v + C2 * q + h) for v, q, h in zip(now[x], now[sq], high)
                ]

            return run

        def second():
            now["m"] = [mm(a, split(b)) for a, b in zip(now["xs"], now["w"])]
            now["ms"] = [split(v) for v in now["m"]]

        def inverse():
            now["i"] = [mm(a, b) for a, b in zip(now["z"], now["q"])]

        def write():
            for (p, g), z, norm in zip(ids, now["i"], now["norm"]):
                near = g * padded(len(POINTS)) + skip + p
                far = g * n + p
                pull = pull_in_ref[near : near + 1, :] + pull_ref[far : far + 1, :]
                inner = jnp.sum(z * pull, 1, keepdims=True)
                shift = jnp.sum(z * inner, 0, keepdims=True) * (1.0 / (norm * (K - 1.0)))
                out_ref[p, g] = (z * (1.0 / jnp.sqrt(norm)) + shift).astype(BF16)

        return [
            gram,
            scale,
            square("xs", "b", mm_high),
            polynomial("x", "b", "z", rounded, mm_high),
            square("z", "w", mm),
            second,
            square("ms", "c", mm),
            polynomial("m", "c", "q", split, mm),
            inverse,
            write,
        ]

    order = []
    for k, first in enumerate(range(0, len(points), batch)):
        order += [(k * LAG + j, k, step) for j, step in enumerate(steps(first))]
    for _, _, step in sorted(order, key=lambda e: e[:2]):
        step()


def specs(n, scalars=1):
    return [pl.BlockSpec(memory_space=pltpu.SMEM)] * scalars + [pl.BlockSpec(memory_space=pltpu.VMEM)] * n


def joined(kernel, rows, name, *blocks):
    return pl.pallas_call(
        kernel,
        out_shape=[jax.ShapeDtypeStruct((n, K), BF16) for n in rows],
        in_specs=specs(len(blocks), 0),
        compiler_params=pltpu.CompilerParams(vmem_limit_bytes=2 << 20),
        name=name,
    )(*blocks)


def near_sums(frame, own, other):
    n = len(POINTS)
    return pl.pallas_call(
        near_kernel,
        out_shape=[
            jax.ShapeDtypeStruct((2 * FIRST, K, K), F32),
            jax.ShapeDtypeStruct((2 * (n - FIRST), K, K), F32),
            jax.ShapeDtypeStruct((2 * padded(n), K), F32),
        ],
        in_specs=specs(2),
        scratch_shapes=sum_scratch(POINTS, (0, 1)),
        compiler_params=pltpu.CompilerParams(vmem_limit_bytes=16 << 20),
        cost_estimate=pl.CostEstimate(flops=6_000_000_000, bytes_accessed=5_000_000, transcendentals=0),
        name="near_sums",
    )(frame, own, other)


def transforms(points, rows, batch, name, frame, *arrays):
    n = len(points)
    return pl.pallas_call(
        functools.partial(points_kernel, points, rows, batch),
        out_shape=jax.ShapeDtypeStruct((n, 2, K, K), BF16),
        in_specs=specs(len(arrays)),
        scratch_shapes=sum_scratch(points, rows)
        + [pltpu.VMEM((2 * n, K, K), F32), pltpu.VMEM((2 * padded(n), K), F32)],
        compiler_params=pltpu.CompilerParams(vmem_limit_bytes=28 << 20),
        cost_estimate=pl.CostEstimate(flops=n * FLOPS, bytes_accessed=4_000_000, transcendentals=0),
        name=name,
    )(frame, *arrays)


def anomalies_kernel(ens_ref, anom_ref, mean_ref):
    ones = jnp.ones((K, K), BF16)
    rows = CT * 2 * NHALF
    for i in range(CT):
        ens = ens_ref[i].reshape(rows, K)
        mean = lax.dot_general(ens, ones, NN, preferred_element_type=F32) * (1.0 / K)
        anom_ref[i] = (ens.astype(F32) - mean).astype(BF16).reshape(CT, 2 * NHALF, K)
        mean_ref[i] = mean.reshape(CT, 2 * NHALF, K)


def anomalies(ensemble):
    return pl.pallas_call(
        anomalies_kernel,
        out_shape=[
            jax.ShapeDtypeStruct(ensemble.shape, BF16),
            jax.ShapeDtypeStruct(ensemble.shape, F32),
        ],
        in_specs=specs(1, 0),
        compiler_params=pltpu.CompilerParams(vmem_limit_bytes=12 << 20),
        cost_estimate=pl.CostEstimate(flops=1_000_000_000, bytes_accessed=4_000_000, transcendentals=0),
        name="anomalies",
    )(ensemble)


def apply_kernel(frame_ref, anom_ref, mean_ref, first_ref, rest_ref, high_ref, out_ref, sum_ref):
    rx, ry, edge = frame_ref[0], frame_ref[1], frame_ref[2]

    def transform(x, y, g):
        if y == 0:
            return first_ref[x + edge * SIDE, g]
        if y < 3:
            return first_ref[y * SIDE + x, g]
        if y <= APX:
            return rest_ref[(y - 3) * SIDE + x, g]
        return high_ref[SIDE - 1 - x, g]

    frac = [(s + 0.5) / SPACING for s in range(SPACING)]
    factor = [[1.0 - f for f in frac], frac]

    def columns(x):
        at = [(i, x - (i + 1) // SPACING, (i + 1) % SPACING) for i in range(CT)]
        return [(i, factor[c][s], c == 1) for i, c, s in at if c in (0, 1)]

    def place(i, j):
        return i + rx * (CT - 1 - 2 * i), j + ry * (CT - 1 - 2 * j)

    for y in range(SIDE):
        for x in range(SIDE):
            cells = [(i, j, fi * fj, li and lj) for i, fi, li in columns(x) for j, fj, lj in columns(y)]
            for g in range(2):
                span = slice(g * NHALF, (g + 1) * NHALF)
                left = jnp.concatenate([anom_ref[(*place(i, j), span)] for i, j, _, _ in cells], 0)
                prod = lax.dot_general(left, transform(x, y, g), NT, preferred_element_type=F32)
                for c, (i, j, share, last) in enumerate(cells):
                    fresh = x == (i + 1) // SPACING and y == (j + 1) // SPACING
                    total = mean_ref[(*place(i, j), span)] if fresh else sum_ref[i, j, span]
                    total = total + prod[c * NHALF : (c + 1) * NHALF] * share
                    if last:
                        out_ref[(*place(i, j), span)] = total.astype(BF16)
                    else:
                        sum_ref[i, j, span] = total


def apply(frame, anom, mean, first, rest, high):
    return pl.pallas_call(
        apply_kernel,
        out_shape=jax.ShapeDtypeStruct(anom.shape, BF16),
        in_specs=specs(5),
        scratch_shapes=[pltpu.VMEM(anom.shape, F32)],
        compiler_params=pltpu.CompilerParams(vmem_limit_bytes=16 << 20),
        name="apply_transforms",
    )(frame, anom, mean, first, rest, high)


def moved(block, source, sizes):
    nx, ny = sizes
    pairs = []
    for x in range(nx):
        for y in range(ny):
            at = source(x, y)
            if at is not None:
                pairs.append((at[0] % nx * ny + at[1], x * ny + y))
    return lax.ppermute(block, ("gx", "gy"), pairs)


def shards(ensemble, obs_anom, obs_innov, obs_prec, obs_pos, obs_count):
    sizes = (lax.axis_size("gx"), lax.axis_size("gy"))

    def core(x, y):
        return x, y ^ 1

    def side(distance):
        return lambda x, y: (x + distance * (1 - 2 * ((x ^ y) & 1)), y)

    def beyond(x, y):
        at = y + 2 * (y & 1) - 1
        return (x, at) if 0 <= at < sizes[1] else None

    own = pl.pallas_call(
        pack_kernel,
        out_shape=jax.ShapeDtypeStruct((ROWS, K), BF16),
        in_specs=specs(4),
        name="pack_slots",
    )(
        obs_count,
        obs_anom.reshape(K, K),
        obs_innov.reshape(1, K),
        obs_prec.reshape(1, K),
        obs_pos.reshape(2, K),
    )
    col, row = lax.axis_index("gx"), lax.axis_index("gy")
    edge = jnp.where((row == 0) | (row == sizes[1] - 1), 1, 0)
    frame = jnp.stack([(col ^ row) & 1, row & 1, edge]).astype(jnp.int32)

    (pair,) = joined(pair_kernel, [PAIR], "pair_tiles", own, moved(own, core, sizes))
    a = moved(pair, side(1), sizes)
    b = moved(pair, side(2), sizes)
    ta = moved(a, core, sizes)
    tb = moved(b, core, sizes)
    near, next_row = joined(rows_kernel, [WIDE, WIDE], "two_rows", pair, a, b, ta, tb)
    y1 = moved(near, beyond, sizes)
    anom, mean = anomalies(ensemble)
    gram_first, gram_rest, pull = near_sums(frame, near, next_row)
    y2 = moved(lax.optimization_barrier((next_row, pull))[0], beyond, sizes)
    z = moved(lax.optimization_barrier((y1, pull))[0], core, sizes)
    rest = transforms(POINTS[FIRST:], (-1, 2), 12, "rest_points", frame, y1, z, gram_rest, pull)
    first = transforms(POINTS[:FIRST], (-2, -1), 9, "first_points", frame, y2, y1, gram_first, pull)
    high = moved(rest[-SIDE:], core, sizes)
    return apply(frame, anom, mean, first, rest, high)


def solution(mesh):
    placed = (
        P("gx", "gy", None, None),
        P("gx", "gy", None, None),
        P("gx", "gy", None),
        P("gx", "gy", None),
        P("gx", "gy", None, None),
        P("gx", "gy"),
    )
    return jax.shard_map(
        shards, mesh=mesh, in_specs=placed, out_specs=P("gx", "gy", None, None), check_vma=False
    )
```

```python
import functools

import jax
import jax.numpy as jnp
from jax import lax
from jax.experimental import pallas as pl
from jax.experimental.pallas import tpu as pltpu
from jax.sharding import PartitionSpec as P

K = 128
APX = 4
CT = 8
SPACING = 2
RLOC = 12
NHALF = 32
META = 4
ROWS = K + 16
PAIR = 2 * K + 16
WIDE = 5 * K + 32
SLOTS = 2
FLOPS = 500_000_000
LAG = 10

NT = (((1,), (1,)), ((), ()))
NN = (((1,), (0,)), ((), ()))
F32 = jnp.float32
BF16 = jnp.bfloat16

SIDE = APX + 2
POINTS = [(a, b) for b in range(-1, APX) for a in range(-1, APX + 1)]
FIRST = 3 * SIDE


def center(a):
    return SPACING * a + (SPACING - 1) / 2.0


def least_distance(offset, point):
    return min(abs(offset * CT + s - center(point)) for s in range(CT))


def tiles_of(point, rows):
    a, b = point
    return [
        (ox, oy)
        for oy in rows
        for ox in range(-2, 3)
        if least_distance(ox, a) ** 2 + least_distance(oy, b) ** 2 < RLOC * RLOC
    ]


def split(x):
    hi = x.astype(BF16)
    lo = (x - hi.astype(F32)).astype(BF16)
    return hi, lo


def mm(a, b):
    left = jnp.concatenate([a[0], a[1]], 1)
    right = jnp.concatenate([b[0], b[1]], 1)
    right = jnp.concatenate([right, right], 0)
    out = lax.dot_general(left, right, NN, preferred_element_type=F32)
    return out[:, :K] + out[:, K:]


def rounded(x):
    return (x.astype(BF16),)


def mm_high(a, b):
    return lax.dot_general(a[0], b[0], NN, preferred_element_type=F32)


C0, C1, C2, C3, C4 = 2.25, -2.4375, 1.6875, -0.5625, 0.0625


def pack_kernel(count_ref, anom_ref, innov_ref, prec_ref, pos_ref, out_ref):
    out_ref[0:K, :] = anom_ref[...].astype(F32).T.astype(BF16)
    slot = lax.broadcasted_iota(jnp.int32, (1, K), 1)
    live = jnp.where(slot < count_ref[0, 0], prec_ref[...].astype(F32), 0.0)
    meta = jnp.concatenate(
        [innov_ref[...].astype(F32), live, pos_ref[...].astype(F32), jnp.zeros((12, K), F32)], 0
    )
    out_ref[K:ROWS, :] = meta.astype(BF16)


def pair_kernel(own_ref, other_ref, out_ref):
    out_ref[0:K, :] = own_ref[0:K, :]
    out_ref[K : 2 * K, :] = other_ref[0:K, :]
    meta = [ref[K:ROWS, :].astype(F32)[0:META] for ref in (own_ref, other_ref)]
    out_ref[2 * K : PAIR, :] = jnp.concatenate(meta + [jnp.zeros((8, K), F32)], 0).astype(BF16)


def rows_kernel(pair_ref, a_ref, b_ref, ta_ref, tb_ref, *out_refs):
    for row, out_ref in enumerate(out_refs):
        parts = [(tb_ref, 1 - row), (ta_ref, 1 - row), (pair_ref, row), (a_ref, row), (b_ref, row)]
        meta = []
        for k, (ref, at) in enumerate(parts):
            out_ref[k * K : k * K + K, :] = ref[at * K : at * K + K, :]
            meta.append(ref[2 * K : PAIR, :].astype(F32)[at * META : at * META + META])
        meta.append(jnp.zeros((12, K), F32))
        out_ref[5 * K : WIDE, :] = jnp.concatenate(meta, 0).astype(BF16)


def padded(n):
    return (n + 7) // 8 * 8


def point_weights(meta, frame_ref, ox, oy, points):
    rows = padded(len(points))
    at = lax.broadcasted_iota(jnp.int32, (rows, K), 0)
    px = jnp.zeros((rows, K), F32)
    py = px
    for i, (a, b) in enumerate(points):
        px = jnp.where(at == i, center(a), px)
        py = jnp.where(at == i, center(b), py)
    rx = frame_ref[0].astype(F32)
    ry = frame_ref[1].astype(F32)
    x = meta[2:3] * (1.0 - 2.0 * rx) + (CT - 1.0) * rx
    y = meta[3:4] * (1.0 - 2.0 * ry) + (CT - 1.0) * ry
    dx = (x + float(ox * CT)) - px
    dy = (y + float(oy * CT)) - py
    sq = dx * dx + dy * dy
    inside = sq < float(RLOC * RLOC)
    out = []
    for rate in (2.0, 4.5):
        out.append(jnp.where(inside, jnp.exp(-sq * (rate / (RLOC * RLOC))), 0.0) * meta[1:2])
    return out


def add_up(points, rows, block, frame_ref, sw_ref, wp_ref, s_ref, put_gram, put_pull):
    seen = sorted({t for p in points for t in tiles_of(p, rows)})
    place = {t: i for i, t in enumerate(seen)}
    n = padded(len(points))

    def anom(t):
        ref, k = block(t)
        return ref[k * K : k * K + K, :]

    metas = {}
    for t in seen:
        ref, k = block(t)
        if id(ref) not in metas:
            metas[id(ref)] = ref[5 * K : WIDE, :].astype(F32)
        meta = metas[id(ref)][k * META : k * META + META]
        w = point_weights(meta, frame_ref, t[0], t[1], points)
        lanes = slice(place[t] * K, place[t] * K + K)
        for g in range(2):
            sw_ref[place[t], g * n : g * n + n, :] = jnp.sqrt(w[g])
        hi, lo = split(jnp.concatenate(w, 0) * meta[0:1])
        wp_ref[0 : 2 * n, lanes] = hi
        wp_ref[2 * n : 4 * n, lanes] = lo
    anom_seen = jnp.concatenate([anom(t) for t in seen], 1)
    pull = lax.dot_general(wp_ref[...], anom_seen, NT, preferred_element_type=F32)
    put_pull(pull[0 : 2 * n] + pull[2 * n : 4 * n])

    def add_point(i):
        own = tiles_of(points[i], rows)
        for j, t in enumerate(own):
            rows_in = anom(t).astype(F32)
            for g in range(2):
                scale = sw_ref[place[t], g * n + i : g * n + i + 1, :]
                s_ref[i % SLOTS, g, :, j * K : j * K + K] = (rows_in * scale).astype(BF16)
        for g in range(2):
            s = s_ref[i % SLOTS, g, :, 0 : len(own) * K]
            put_gram(i, g, lax.dot_general(s, s, NT, preferred_element_type=F32))

    return add_point


def sum_scratch(points, rows):
    n = padded(len(points))
    seen = len({t for p in points for t in tiles_of(p, rows)})
    most = max(len(tiles_of(p, rows)) for p in points)
    return [
        pltpu.VMEM((seen, 2 * n, K), F32),
        pltpu.VMEM((4 * n, seen * K), BF16),
        pltpu.VMEM((SLOTS, 2, K, most * K), BF16),
    ]


def near_kernel(frame_ref, own_ref, other_ref, first_ref, rest_ref, pull_ref, *scratch):
    def block(t):
        return (own_ref, other_ref)[t[1]], 2 + t[0]

    def put_gram(i, g, value):
        if i < FIRST:
            first_ref[2 * i + g] = value
        else:
            rest_ref[2 * (i - FIRST) + g] = value

    def put_pull(value):
        pull_ref[...] = value

    add_point = add_up(POINTS, (0, 1), block, frame_ref, *scratch, put_gram, put_pull)
    for i in range(len(POINTS)):
        add_point(i)


def points_kernel(points, rows, batch, *refs):
    frame_ref = refs[0]
    row_refs = dict(zip(rows, refs[1:]))
    gram_ref, pull_in_ref, out_ref, sw, wp, s, g_ref, pull_ref = refs[-8:]
    n = padded(len(points))
    skip = POINTS.index(points[0])

    def block(t):
        ox, oy = t
        return row_refs[oy], 2 + (-ox if oy == -1 else ox)

    def put_gram(i, g, value):
        g_ref[2 * i + g] = gram_ref[2 * i + g] + value

    def put_pull(value):
        pull_ref[...] = value

    add_point = add_up(points, rows, block, frame_ref, sw, wp, s, put_gram, put_pull)
    row = lax.broadcasted_iota(jnp.int32, (K, K), 0)
    col = lax.broadcasted_iota(jnp.int32, (K, K), 1)
    eye = jnp.where(row == col, 1.0, 0.0).astype(F32)

    def steps(first):
        ids = [(p, g) for p in range(first, min(first + batch, len(points))) for g in range(2)]
        now = {}

        def gram():
            for p, g in ids[::2]:
                add_point(p)

        def scale():
            now["x"], now["norm"] = [], []
            for p, g in ids:
                system = eye + g_ref[2 * p + g] * (1.0 / (K - 1.0))
                sq = jnp.sum(jnp.sum(system * system, 0, keepdims=True), 1, keepdims=True)
                norm = jnp.sqrt(sq)
                now["norm"].append(norm)
                now["x"].append(system * (1.0 / norm))
            now["xs"] = [split(x) for x in now["x"]]

        def square(parts, out, times):
            def run():
                now[out] = [times(v, v) for v in now[parts]]

            return run

        def polynomial(x, sq, out, parts, times):
            def run():
                high = [times(parts(q), parts(C3 * v + C4 * q)) for v, q in zip(now[x], now[sq])]
                now[out] = [
                    split(C0 * eye + C1 * v + C2 * q + h) for v, q, h in zip(now[x], now[sq], high)
                ]

            return run

        def second():
            now["m"] = [mm(a, split(b)) for a, b in zip(now["xs"], now["w"])]
            now["ms"] = [split(v) for v in now["m"]]

        def inverse():
            now["i"] = [mm(a, b) for a, b in zip(now["z"], now["q"])]

        def write():
            for (p, g), z, norm in zip(ids, now["i"], now["norm"]):
                near = g * padded(len(POINTS)) + skip + p
                far = g * n + p
                pull = pull_in_ref[near : near + 1, :] + pull_ref[far : far + 1, :]
                inner = jnp.sum(z * pull, 1, keepdims=True)
                shift = jnp.sum(z * inner, 0, keepdims=True) * (1.0 / (norm * (K - 1.0)))
                out_ref[p, g] = (z * (1.0 / jnp.sqrt(norm)) + shift).astype(BF16)

        return [
            gram,
            scale,
            square("xs", "b", mm_high),
            polynomial("x", "b", "z", rounded, mm_high),
            square("z", "w", mm),
            second,
            square("ms", "c", mm),
            polynomial("m", "c", "q", split, mm),
            inverse,
            write,
        ]

    order = []
    for k, first in enumerate(range(0, len(points), batch)):
        order += [(k * LAG + j, k, step) for j, step in enumerate(steps(first))]
    for _, _, step in sorted(order, key=lambda e: e[:2]):
        step()


def specs(n, scalars=1):
    return [pl.BlockSpec(memory_space=pltpu.SMEM)] * scalars + [pl.BlockSpec(memory_space=pltpu.VMEM)] * n


def joined(kernel, rows, name, *blocks):
    return pl.pallas_call(
        kernel,
        out_shape=[jax.ShapeDtypeStruct((n, K), BF16) for n in rows],
        in_specs=specs(len(blocks), 0),
        compiler_params=pltpu.CompilerParams(vmem_limit_bytes=2 << 20),
        name=name,
    )(*blocks)


def near_sums(frame, own, other):
    n = len(POINTS)
    return pl.pallas_call(
        near_kernel,
        out_shape=[
            jax.ShapeDtypeStruct((2 * FIRST, K, K), F32),
            jax.ShapeDtypeStruct((2 * (n - FIRST), K, K), F32),
            jax.ShapeDtypeStruct((2 * padded(n), K), F32),
        ],
        in_specs=specs(2),
        scratch_shapes=sum_scratch(POINTS, (0, 1)),
        compiler_params=pltpu.CompilerParams(vmem_limit_bytes=12 << 20),
        cost_estimate=pl.CostEstimate(flops=6_000_000_000, bytes_accessed=5_000_000, transcendentals=0),
        name="near_sums",
    )(frame, own, other)


def transforms(points, rows, batch, name, frame, *arrays):
    n = len(points)
    return pl.pallas_call(
        functools.partial(points_kernel, points, rows, batch),
        out_shape=jax.ShapeDtypeStruct((n, 2, K, K), BF16),
        in_specs=specs(len(arrays)),
        scratch_shapes=sum_scratch(points, rows)
        + [pltpu.VMEM((2 * n, K, K), F32), pltpu.VMEM((2 * padded(n), K), F32)],
        compiler_params=pltpu.CompilerParams(vmem_limit_bytes=16 << 20),
        cost_estimate=pl.CostEstimate(flops=n * FLOPS, bytes_accessed=4_000_000, transcendentals=0),
        name=name,
    )(frame, *arrays)


def anomalies_kernel(ens_ref, anom_ref, mean_ref):
    ones = jnp.ones((K, K), BF16)
    rows = CT * 2 * NHALF
    for i in range(CT):
        ens = ens_ref[i].reshape(rows, K)
        mean = lax.dot_general(ens, ones, NN, preferred_element_type=F32) * (1.0 / K)
        anom_ref[i] = (ens.astype(F32) - mean).astype(BF16).reshape(CT, 2 * NHALF, K)
        mean_ref[i] = mean.reshape(CT, 2 * NHALF, K)


def anomalies(ensemble):
    return pl.pallas_call(
        anomalies_kernel,
        out_shape=[
            jax.ShapeDtypeStruct(ensemble.shape, BF16),
            jax.ShapeDtypeStruct(ensemble.shape, F32),
        ],
        in_specs=specs(1, 0),
        compiler_params=pltpu.CompilerParams(vmem_limit_bytes=12 << 20),
        cost_estimate=pl.CostEstimate(flops=1_000_000_000, bytes_accessed=4_000_000, transcendentals=0),
        name="anomalies",
    )(ensemble)


def apply_kernel(frame_ref, anom_ref, mean_ref, first_ref, rest_ref, high_ref, out_ref, sum_ref):
    rx, ry, edge = frame_ref[0], frame_ref[1], frame_ref[2]

    def transform(x, y, g):
        if y == 0:
            return first_ref[x + edge * SIDE, g]
        if y < 3:
            return first_ref[y * SIDE + x, g]
        if y <= APX:
            return rest_ref[(y - 3) * SIDE + x, g]
        return high_ref[SIDE - 1 - x, g]

    frac = [(s + 0.5) / SPACING for s in range(SPACING)]
    factor = [[1.0 - f for f in frac], frac]

    def columns(x):
        at = [(i, x - (i + 1) // SPACING, (i + 1) % SPACING) for i in range(CT)]
        return [(i, factor[c][s], c == 1) for i, c, s in at if c in (0, 1)]

    def place(i, j):
        return i + rx * (CT - 1 - 2 * i), j + ry * (CT - 1 - 2 * j)

    for y in range(SIDE):
        for x in range(SIDE):
            cells = [(i, j, fi * fj, li and lj) for i, fi, li in columns(x) for j, fj, lj in columns(y)]
            for g in range(2):
                span = slice(g * NHALF, (g + 1) * NHALF)
                left = jnp.concatenate([anom_ref[(*place(i, j), span)] for i, j, _, _ in cells], 0)
                prod = lax.dot_general(left, transform(x, y, g), NT, preferred_element_type=F32)
                for c, (i, j, share, last) in enumerate(cells):
                    fresh = x == (i + 1) // SPACING and y == (j + 1) // SPACING
                    total = mean_ref[(*place(i, j), span)] if fresh else sum_ref[i, j, span]
                    total = total + prod[c * NHALF : (c + 1) * NHALF] * share
                    if last:
                        out_ref[(*place(i, j), span)] = total.astype(BF16)
                    else:
                        sum_ref[i, j, span] = total


def apply(frame, anom, mean, first, rest, high):
    return pl.pallas_call(
        apply_kernel,
        out_shape=jax.ShapeDtypeStruct(anom.shape, BF16),
        in_specs=specs(5),
        scratch_shapes=[pltpu.VMEM(anom.shape, F32)],
        compiler_params=pltpu.CompilerParams(vmem_limit_bytes=16 << 20),
        name="apply_transforms",
    )(frame, anom, mean, first, rest, high)


def moved(block, source, sizes):
    nx, ny = sizes
    pairs = []
    for x in range(nx):
        for y in range(ny):
            at = source(x, y)
            if at is not None:
                pairs.append((at[0] % nx * ny + at[1], x * ny + y))
    return lax.ppermute(block, ("gx", "gy"), pairs)


def shards(ensemble, obs_anom, obs_innov, obs_prec, obs_pos, obs_count):
    sizes = (lax.axis_size("gx"), lax.axis_size("gy"))

    def core(x, y):
        return x, y ^ 1

    def side(distance):
        return lambda x, y: (x + distance * (1 - 2 * ((x ^ y) & 1)), y)

    def beyond(x, y):
        at = y + 2 * (y & 1) - 1
        return (x, at) if 0 <= at < sizes[1] else None

    def across(x, y):
        at = y + 3 - 6 * (y & 1)
        return (x, at) if 0 <= at < sizes[1] else None

    own = pl.pallas_call(
        pack_kernel,
        out_shape=jax.ShapeDtypeStruct((ROWS, K), BF16),
        in_specs=specs(4),
        name="pack_slots",
    )(
        obs_count,
        obs_anom.reshape(K, K),
        obs_innov.reshape(1, K),
        obs_prec.reshape(1, K),
        obs_pos.reshape(2, K),
    )
    col, row = lax.axis_index("gx"), lax.axis_index("gy")
    edge = jnp.where((row == 0) | (row == sizes[1] - 1), 1, 0)
    frame = jnp.stack([(col ^ row) & 1, row & 1, edge]).astype(jnp.int32)

    (pair,) = joined(pair_kernel, [PAIR], "pair_tiles", own, moved(own, core, sizes))
    a = moved(pair, side(1), sizes)
    b = moved(pair, side(2), sizes)
    ta = moved(a, core, sizes)
    tb = moved(b, core, sizes)
    near, next_row = joined(rows_kernel, [WIDE, WIDE], "two_rows", pair, a, b, ta, tb)
    y1 = moved(near, beyond, sizes)
    anom, mean = anomalies(ensemble)
    gram_first, gram_rest, pull = near_sums(frame, near, next_row)
    y2 = moved(near, across, sizes)
    y1, pull = lax.optimization_barrier((y1, pull))
    z1 = lax.cond(obs_count[0, 0] >= 0, lambda v: moved(v, core, sizes), lambda v: v, y1)
    rest = transforms(POINTS[FIRST:], (-1, 2), 12, "rest_points", frame, y1, z1, gram_rest, pull)
    z2 = moved(lax.optimization_barrier((y2, rest))[0], core, sizes)
    first = transforms(POINTS[:FIRST], (-2, -1), 9, "first_points", frame, z2, y1, gram_first, pull)
    high = moved(rest[-SIDE:], core, sizes)
    return apply(frame, anom, mean, first, rest, high)


def solution(mesh):
    placed = (
        P("gx", "gy", None, None),
        P("gx", "gy", None, None),
        P("gx", "gy", None),
        P("gx", "gy", None),
        P("gx", "gy", None, None),
        P("gx", "gy"),
    )
    return jax.shard_map(
        shards, mesh=mesh, in_specs=placed, out_specs=P("gx", "gy", None, None), check_vma=False
    )
```

```python
import functools

import jax
import jax.numpy as jnp
from jax import lax
from jax.experimental import pallas as pl
from jax.experimental.pallas import tpu as pltpu
from jax.sharding import PartitionSpec as P

K = 128
APX = 4
CT = 8
SPACING = 2
RLOC = 12
NHALF = 32
META = 4
ROWS = K + 16
PAIR = 2 * K + 16
WIDE = 5 * K + 32
ORDER = (-2, 2, -1, 0, 1)
EDGES = 2
SLOTS = 2
REST = 1_000_000
LAG = 10

NT = (((1,), (1,)), ((), ()))
NN = (((1,), (0,)), ((), ()))
F32 = jnp.float32
BF16 = jnp.bfloat16

SIDE = APX + 2
POINTS = [(a, b) for b in range(-1, APX) for a in range(-1, APX + 1)]
FIRST = 3 * SIDE


def center(a):
    return SPACING * a + (SPACING - 1) / 2.0


def least_distance(offset, point):
    return min(abs(offset * CT + s - center(point)) for s in range(CT))


def tiles_of(point, rows):
    a, b = point
    return [
        (ox, oy)
        for oy in rows
        for ox in range(-2, 3)
        if least_distance(ox, a) ** 2 + least_distance(oy, b) ** 2 < RLOC * RLOC
    ]


def split(x):
    hi = x.astype(BF16)
    lo = (x - hi.astype(F32)).astype(BF16)
    return hi, lo


def mm(a, b):
    left = jnp.concatenate([a[0], a[1]], 1)
    right = jnp.concatenate([b[0], b[1]], 1)
    right = jnp.concatenate([right, right], 0)
    out = lax.dot_general(left, right, NN, preferred_element_type=F32)
    return out[:, :K] + out[:, K:]


def rounded(x):
    return (x.astype(BF16),)


def mm_high(a, b):
    return lax.dot_general(a[0], b[0], NN, preferred_element_type=F32)


C0, C1, C2, C3, C4 = 2.25, -2.4375, 1.6875, -0.5625, 0.0625


def pack_kernel(count_ref, anom_ref, innov_ref, prec_ref, pos_ref, out_ref):
    out_ref[0:K, :] = anom_ref[...].astype(F32).T.astype(BF16)
    slot = lax.broadcasted_iota(jnp.int32, (1, K), 1)
    live = jnp.where(slot < count_ref[0, 0], prec_ref[...].astype(F32), 0.0)
    meta = jnp.concatenate(
        [innov_ref[...].astype(F32), live, pos_ref[...].astype(F32), jnp.zeros((12, K), F32)], 0
    )
    out_ref[K:ROWS, :] = meta.astype(BF16)


def pair_kernel(own_ref, other_ref, out_ref):
    out_ref[0:K, :] = own_ref[0:K, :]
    out_ref[K : 2 * K, :] = other_ref[0:K, :]
    meta = [ref[K:ROWS, :].astype(F32)[0:META] for ref in (own_ref, other_ref)]
    out_ref[2 * K : PAIR, :] = jnp.concatenate(meta + [jnp.zeros((8, K), F32)], 0).astype(BF16)


def rows_kernel(pair_ref, a_ref, b_ref, ta_ref, tb_ref, *out_refs):
    for row, out_ref in enumerate(out_refs):
        parts = [(tb_ref, 1 - row), (b_ref, row), (ta_ref, 1 - row), (pair_ref, row), (a_ref, row)]
        meta = []
        for k, (ref, at) in enumerate(parts):
            out_ref[k * K : k * K + K, :] = ref[at * K : at * K + K, :]
            meta.append(ref[2 * K : PAIR, :].astype(F32)[at * META : at * META + META])
        meta.append(jnp.zeros((12, K), F32))
        out_ref[5 * K : WIDE, :] = jnp.concatenate(meta, 0).astype(BF16)


def padded(n):
    return (n + 7) // 8 * 8


def point_weights(meta, frame_ref, ox, oy, points):
    rows = padded(len(points))
    at = lax.broadcasted_iota(jnp.int32, (rows, K), 0)
    px = jnp.zeros((rows, K), F32)
    py = px
    for i, (a, b) in enumerate(points):
        px = jnp.where(at == i, center(a), px)
        py = jnp.where(at == i, center(b), py)
    rx = frame_ref[0].astype(F32)
    ry = frame_ref[1].astype(F32)
    x = meta[2:3] * (1.0 - 2.0 * rx) + (CT - 1.0) * rx
    y = meta[3:4] * (1.0 - 2.0 * ry) + (CT - 1.0) * ry
    dx = (x + float(ox * CT)) - px
    dy = (y + float(oy * CT)) - py
    sq = dx * dx + dy * dy
    inside = sq < float(RLOC * RLOC)
    out = []
    for rate in (2.0, 4.5):
        out.append(jnp.where(inside, jnp.exp(-sq * (rate / (RLOC * RLOC))), 0.0) * meta[1:2])
    return out


def add_up(points, rows, block, frame_ref, sw_ref, wp_ref, s_ref, put_gram, put_pull):
    seen = sorted({t for p in points for t in tiles_of(p, rows)})
    place = {t: i for i, t in enumerate(seen)}
    n = padded(len(points))

    def anom(t):
        ref, ox = block(t)
        k = ORDER.index(ox) - (WIDE - ref.shape[0]) // K
        return ref[k * K : k * K + K, :]

    metas = {}
    for t in seen:
        ref, ox = block(t)
        if id(ref) not in metas:
            metas[id(ref)] = ref[ref.shape[0] - 32 :, :].astype(F32)
        k = ORDER.index(ox)
        meta = metas[id(ref)][k * META : k * META + META]
        w = point_weights(meta, frame_ref, t[0], t[1], points)
        lanes = slice(place[t] * K, place[t] * K + K)
        for g in range(2):
            sw_ref[place[t], g * n : g * n + n, :] = jnp.sqrt(w[g])
        hi, lo = split(jnp.concatenate(w, 0) * meta[0:1])
        wp_ref[0 : 2 * n, lanes] = hi
        wp_ref[2 * n : 4 * n, lanes] = lo
    anom_seen = jnp.concatenate([anom(t) for t in seen], 1)
    pull = lax.dot_general(wp_ref[...], anom_seen, NT, preferred_element_type=F32)
    put_pull(pull[0 : 2 * n] + pull[2 * n : 4 * n])

    def add_point(i):
        own = tiles_of(points[i], rows)
        for j, t in enumerate(own):
            rows_in = anom(t).astype(F32)
            for g in range(2):
                scale = sw_ref[place[t], g * n + i : g * n + i + 1, :]
                s_ref[i % SLOTS, g, :, j * K : j * K + K] = (rows_in * scale).astype(BF16)
        for g in range(2):
            s = s_ref[i % SLOTS, g, :, 0 : len(own) * K]
            put_gram(i, g, lax.dot_general(s, s, NT, preferred_element_type=F32))

    return add_point


def sum_scratch(points, rows):
    n = padded(len(points))
    seen = len({t for p in points for t in tiles_of(p, rows)})
    most = max(len(tiles_of(p, rows)) for p in points)
    return [
        pltpu.VMEM((seen, 2 * n, K), F32),
        pltpu.VMEM((4 * n, seen * K), BF16),
        pltpu.VMEM((SLOTS, 2, K, most * K), BF16),
    ]


def near_kernel(frame_ref, own_ref, other_ref, first_ref, rest_ref, pull_ref, *scratch):
    def block(t):
        return (own_ref, other_ref)[t[1]], t[0]

    def put_gram(i, g, value):
        if i < FIRST:
            first_ref[2 * i + g] = value
        else:
            rest_ref[2 * (i - FIRST) + g] = value

    def put_pull(value):
        pull_ref[...] = value

    add_point = add_up(POINTS, (0, 1), block, frame_ref, *scratch, put_gram, put_pull)
    for i in range(len(POINTS)):
        add_point(i)


def points_kernel(points, rows, batch, *refs):
    frame_ref = refs[0]
    row_refs = dict(zip(rows, refs[1:]))
    gram_ref, pull_in_ref, out_ref, sw, wp, s, g_ref, pull_ref = refs[-8:]
    n = padded(len(points))
    skip = POINTS.index(points[0])

    def block(t):
        ox, oy = t
        return row_refs[oy], -ox if oy == -1 else ox

    def put_gram(i, g, value):
        g_ref[2 * i + g] = gram_ref[2 * i + g] + value

    def put_pull(value):
        pull_ref[...] = value

    add_point = add_up(points, rows, block, frame_ref, sw, wp, s, put_gram, put_pull)
    row = lax.broadcasted_iota(jnp.int32, (K, K), 0)
    col = lax.broadcasted_iota(jnp.int32, (K, K), 1)
    eye = jnp.where(row == col, 1.0, 0.0).astype(F32)

    def steps(first):
        ids = [(p, g) for p in range(first, min(first + batch, len(points))) for g in range(2)]
        now = {}

        def gram():
            for p, g in ids[::2]:
                add_point(p)

        def scale():
            now["x"], now["norm"] = [], []
            for p, g in ids:
                system = eye + g_ref[2 * p + g] * (1.0 / (K - 1.0))
                sq = jnp.sum(jnp.sum(system * system, 0, keepdims=True), 1, keepdims=True)
                norm = jnp.sqrt(sq)
                now["norm"].append(norm)
                now["x"].append(system * (1.0 / norm))
            now["xs"] = [split(x) for x in now["x"]]

        def square(parts, out, times):
            def run():
                now[out] = [times(v, v) for v in now[parts]]

            return run

        def polynomial(x, sq, out, parts, times):
            def run():
                high = [times(parts(q), parts(C3 * v + C4 * q)) for v, q in zip(now[x], now[sq])]
                now[out] = [
                    split(C0 * eye + C1 * v + C2 * q + h) for v, q, h in zip(now[x], now[sq], high)
                ]

            return run

        def second():
            now["m"] = [mm(a, split(b)) for a, b in zip(now["xs"], now["w"])]
            now["ms"] = [split(v) for v in now["m"]]

        def inverse():
            now["i"] = [mm(a, b) for a, b in zip(now["z"], now["q"])]

        def write():
            for (p, g), z, norm in zip(ids, now["i"], now["norm"]):
                near = g * padded(len(POINTS)) + skip + p
                far = g * n + p
                pull = pull_in_ref[near : near + 1, :] + pull_ref[far : far + 1, :]
                inner = jnp.sum(z * pull, 1, keepdims=True)
                shift = jnp.sum(z * inner, 0, keepdims=True) * (1.0 / (norm * (K - 1.0)))
                out_ref[p, g] = (z * (1.0 / jnp.sqrt(norm)) + shift).astype(BF16)

        return [
            gram,
            scale,
            square("xs", "b", mm_high),
            polynomial("x", "b", "z", rounded, mm_high),
            square("z", "w", mm),
            second,
            square("ms", "c", mm),
            polynomial("m", "c", "q", split, mm),
            inverse,
            write,
        ]

    order = []
    for k, first in enumerate(range(0, len(points), batch)):
        order += [(k * LAG + j, k, step) for j, step in enumerate(steps(first))]
    for _, _, step in sorted(order, key=lambda e: e[:2]):
        step()


def specs(n, scalars=1):
    return [pl.BlockSpec(memory_space=pltpu.SMEM)] * scalars + [pl.BlockSpec(memory_space=pltpu.VMEM)] * n


def joined(kernel, rows, name, *blocks):
    return pl.pallas_call(
        kernel,
        out_shape=[jax.ShapeDtypeStruct((n, K), BF16) for n in rows],
        in_specs=specs(len(blocks), 0),
        compiler_params=pltpu.CompilerParams(vmem_limit_bytes=2 << 20),
        name=name,
    )(*blocks)


def near_sums(frame, own, other):
    n = len(POINTS)
    return pl.pallas_call(
        near_kernel,
        out_shape=[
            jax.ShapeDtypeStruct((2 * FIRST, K, K), F32),
            jax.ShapeDtypeStruct((2 * (n - FIRST), K, K), F32),
            jax.ShapeDtypeStruct((2 * padded(n), K), F32),
        ],
        in_specs=specs(2),
        scratch_shapes=sum_scratch(POINTS, (0, 1)),
        compiler_params=pltpu.CompilerParams(vmem_limit_bytes=16 << 20),
        cost_estimate=pl.CostEstimate(flops=6_000_000_000, bytes_accessed=5_000_000, transcendentals=0),
        name="near_sums",
    )(frame, own, other)


def transforms(points, rows, batch, flops, name, frame, *arrays):
    n = len(points)
    return pl.pallas_call(
        functools.partial(points_kernel, points, rows, batch),
        out_shape=jax.ShapeDtypeStruct((n, 2, K, K), BF16),
        in_specs=specs(len(arrays)),
        scratch_shapes=sum_scratch(points, rows)
        + [pltpu.VMEM((2 * n, K, K), F32), pltpu.VMEM((2 * padded(n), K), F32)],
        compiler_params=pltpu.CompilerParams(vmem_limit_bytes=28 << 20),
        cost_estimate=pl.CostEstimate(flops=flops, bytes_accessed=flops // 1000, transcendentals=0),
        name=name,
    )(frame, *arrays)


def anomalies_kernel(ens_ref, anom_ref, mean_ref):
    ones = jnp.ones((K, K), BF16)
    rows = CT * 2 * NHALF
    for i in range(CT):
        ens = ens_ref[i].reshape(rows, K)
        mean = lax.dot_general(ens, ones, NN, preferred_element_type=F32) * (1.0 / K)
        anom_ref[i] = (ens.astype(F32) - mean).astype(BF16).reshape(CT, 2 * NHALF, K)
        mean_ref[i] = mean.reshape(CT, 2 * NHALF, K)


def anomalies(ensemble):
    return pl.pallas_call(
        anomalies_kernel,
        out_shape=[
            jax.ShapeDtypeStruct(ensemble.shape, BF16),
            jax.ShapeDtypeStruct(ensemble.shape, F32),
        ],
        in_specs=specs(1, 0),
        compiler_params=pltpu.CompilerParams(vmem_limit_bytes=12 << 20),
        cost_estimate=pl.CostEstimate(flops=1_000_000_000, bytes_accessed=4_000_000, transcendentals=0),
        name="anomalies",
    )(ensemble)


def apply_kernel(frame_ref, anom_ref, mean_ref, first_ref, rest_ref, high_ref, out_ref, sum_ref):
    rx, ry, edge = frame_ref[0], frame_ref[1], frame_ref[2]

    def transform(x, y, g):
        if y == 0:
            return first_ref[x + edge * SIDE, g]
        if y < 3:
            return first_ref[y * SIDE + x, g]
        if y <= APX:
            return rest_ref[(y - 3) * SIDE + x, g]
        return high_ref[SIDE - 1 - x, g]

    frac = [(s + 0.5) / SPACING for s in range(SPACING)]
    factor = [[1.0 - f for f in frac], frac]

    def columns(x):
        at = [(i, x - (i + 1) // SPACING, (i + 1) % SPACING) for i in range(CT)]
        return [(i, factor[c][s], c == 1) for i, c, s in at if c in (0, 1)]

    def place(i, j):
        return i + rx * (CT - 1 - 2 * i), j + ry * (CT - 1 - 2 * j)

    for y in range(SIDE):
        for x in range(SIDE):
            cells = [(i, j, fi * fj, li and lj) for i, fi, li in columns(x) for j, fj, lj in columns(y)]
            for g in range(2):
                span = slice(g * NHALF, (g + 1) * NHALF)
                left = jnp.concatenate([anom_ref[(*place(i, j), span)] for i, j, _, _ in cells], 0)
                prod = lax.dot_general(left, transform(x, y, g), NT, preferred_element_type=F32)
                for c, (i, j, share, last) in enumerate(cells):
                    fresh = x == (i + 1) // SPACING and y == (j + 1) // SPACING
                    total = mean_ref[(*place(i, j), span)] if fresh else sum_ref[i, j, span]
                    total = total + prod[c * NHALF : (c + 1) * NHALF] * share
                    if last:
                        out_ref[(*place(i, j), span)] = total.astype(BF16)
                    else:
                        sum_ref[i, j, span] = total


def apply(frame, anom, mean, first, rest, high):
    return pl.pallas_call(
        apply_kernel,
        out_shape=jax.ShapeDtypeStruct(anom.shape, BF16),
        in_specs=specs(5),
        scratch_shapes=[pltpu.VMEM(anom.shape, F32)],
        compiler_params=pltpu.CompilerParams(vmem_limit_bytes=16 << 20),
        name="apply_transforms",
    )(frame, anom, mean, first, rest, high)


def moved(block, source, sizes):
    nx, ny = sizes
    pairs = []
    for x in range(nx):
        for y in range(ny):
            at = source(x, y)
            if at is not None:
                pairs.append((at[0] % nx * ny + at[1], x * ny + y))
    return lax.ppermute(block, ("gx", "gy"), pairs)


def shards(ensemble, obs_anom, obs_innov, obs_prec, obs_pos, obs_count):
    sizes = (lax.axis_size("gx"), lax.axis_size("gy"))

    def core(x, y):
        return x, y ^ 1

    def side(distance):
        return lambda x, y: (x + distance * (1 - 2 * ((x ^ y) & 1)), y)

    def beyond(x, y):
        at = y + 2 * (y & 1) - 1
        return (x, at) if 0 <= at < sizes[1] else None

    def across(x, y):
        at = y + 3 - 6 * (y & 1)
        return (x, at) if 0 <= at < sizes[1] else None

    own = pl.pallas_call(
        pack_kernel,
        out_shape=jax.ShapeDtypeStruct((ROWS, K), BF16),
        in_specs=specs(4),
        name="pack_slots",
    )(
        obs_count,
        obs_anom.reshape(K, K),
        obs_innov.reshape(1, K),
        obs_prec.reshape(1, K),
        obs_pos.reshape(2, K),
    )
    col, row = lax.axis_index("gx"), lax.axis_index("gy")
    edge = jnp.where((row == 0) | (row == sizes[1] - 1), 1, 0)
    frame = jnp.stack([(col ^ row) & 1, row & 1, edge]).astype(jnp.int32)

    (pair,) = joined(pair_kernel, [PAIR], "pair_tiles", own, moved(own, core, sizes))
    a = moved(pair, side(1), sizes)
    b = moved(pair, side(2), sizes)
    ta = moved(a, core, sizes)
    tb = moved(b, core, sizes)
    near, next_row = joined(rows_kernel, [WIDE, WIDE], "two_rows", pair, a, b, ta, tb)
    y1 = moved(near, beyond, sizes)
    anom, mean = anomalies(ensemble)
    gram_first, gram_rest, pull = near_sums(frame, near, next_row)
    y2 = moved(near, across, sizes)
    z1 = moved(lax.optimization_barrier((y1, pull))[0][EDGES * K :], core, sizes)
    rest = transforms(POINTS[FIRST:], (-1, 2), 12, REST, "rest_points", frame, y1, z1, gram_rest, pull)
    z2 = moved(lax.optimization_barrier((y2, rest))[0], core, sizes)
    first = transforms(POINTS[:FIRST], (-2, -1), 9, 9_000_000_000, "first_points", frame, z2, y1, gram_first, pull)
    high = moved(rest[-SIDE:], core, sizes)
    return apply(frame, anom, mean, first, rest, high)


def solution(mesh):
    placed = (
        P("gx", "gy", None, None),
        P("gx", "gy", None, None),
        P("gx", "gy", None),
        P("gx", "gy", None),
        P("gx", "gy", None, None),
        P("gx", "gy"),
    )
    return jax.shard_map(
        shards, mesh=mesh, in_specs=placed, out_specs=P("gx", "gy", None, None), check_vma=False
    )
```

```python
import functools

import jax
import jax.numpy as jnp
from jax import lax
from jax.experimental import pallas as pl
from jax.experimental.pallas import tpu as pltpu
from jax.sharding import PartitionSpec as P

K = 128
APX = 4
CT = 8
SPACING = 2
RLOC = 12
NHALF = 32
META = 4
ROWS = K + 16
PAIR = 2 * K + 16
WIDE = 5 * K + 32
ORDER = (-2, 2, -1, 0, 1)
EDGES = 2
SLOTS = 2
REST = 1_000_000
LAG = 10

NT = (((1,), (1,)), ((), ()))
NN = (((1,), (0,)), ((), ()))
F32 = jnp.float32
BF16 = jnp.bfloat16

SIDE = APX + 2
POINTS = [(a, b) for b in range(-1, APX) for a in range(-1, APX + 1)]
FIRST = 3 * SIDE


def center(a):
    return SPACING * a + (SPACING - 1) / 2.0


def least_distance(offset, point):
    return min(abs(offset * CT + s - center(point)) for s in range(CT))


def tiles_of(point, rows):
    a, b = point
    return [
        (ox, oy)
        for oy in rows
        for ox in range(-2, 3)
        if least_distance(ox, a) ** 2 + least_distance(oy, b) ** 2 < RLOC * RLOC
    ]


def split(x):
    hi = x.astype(BF16)
    lo = (x - hi.astype(F32)).astype(BF16)
    return hi, lo


def mm(a, b):
    left = jnp.concatenate([a[0], a[1]], 1)
    right = jnp.concatenate([b[0], b[1]], 1)
    right = jnp.concatenate([right, right], 0)
    out = lax.dot_general(left, right, NN, preferred_element_type=F32)
    return out[:, :K] + out[:, K:]


def rounded(x):
    return (x.astype(BF16),)


def mm_high(a, b):
    return lax.dot_general(a[0], b[0], NN, preferred_element_type=F32)


C0, C1, C2, C3, C4 = 2.25, -2.4375, 1.6875, -0.5625, 0.0625


def pack_kernel(count_ref, anom_ref, innov_ref, prec_ref, pos_ref, out_ref):
    out_ref[0:K, :] = anom_ref[...].astype(F32).T.astype(BF16)
    slot = lax.broadcasted_iota(jnp.int32, (1, K), 1)
    live = jnp.where(slot < count_ref[0, 0], prec_ref[...].astype(F32), 0.0)
    meta = jnp.concatenate(
        [innov_ref[...].astype(F32), live, pos_ref[...].astype(F32), jnp.zeros((12, K), F32)], 0
    )
    out_ref[K:ROWS, :] = meta.astype(BF16)


def pair_kernel(own_ref, other_ref, out_ref):
    out_ref[0:K, :] = own_ref[0:K, :]
    out_ref[K : 2 * K, :] = other_ref[0:K, :]
    meta = [ref[K:ROWS, :].astype(F32)[0:META] for ref in (own_ref, other_ref)]
    out_ref[2 * K : PAIR, :] = jnp.concatenate(meta + [jnp.zeros((8, K), F32)], 0).astype(BF16)


def rows_kernel(frame_ref, pair_ref, a_ref, b_ref, ta_ref, tb_ref, *out_refs):
    same = frame_ref[3] != 0
    for row, out_ref in enumerate(out_refs):
        ends = [(tb_ref, 1 - row), (b_ref, row)]
        middle = [(ta_ref, 1 - row), (pair_ref, row), (a_ref, row)]

        def tile(part):
            return part[0][part[1] * K : part[1] * K + K, :]

        def info(part):
            at = part[1] * META
            return part[0][2 * K : PAIR, :].astype(F32)[at : at + META]

        meta = []
        for k, (left, right) in enumerate((ends, ends[::-1])):
            out_ref[k * K : k * K + K, :] = jnp.where(same, tile(left), tile(right))
            meta.append(jnp.where(same, info(left), info(right)))
        for k, part in enumerate(middle, 2):
            out_ref[k * K : k * K + K, :] = tile(part)
            meta.append(info(part))
        meta.append(jnp.zeros((12, K), F32))
        out_ref[5 * K : WIDE, :] = jnp.concatenate(meta, 0).astype(BF16)


def padded(n):
    return (n + 7) // 8 * 8


def point_weights(meta, frame_ref, ox, oy, points):
    rows = padded(len(points))
    at = lax.broadcasted_iota(jnp.int32, (rows, K), 0)
    px = jnp.zeros((rows, K), F32)
    py = px
    for i, (a, b) in enumerate(points):
        px = jnp.where(at == i, center(a), px)
        py = jnp.where(at == i, center(b), py)
    rx = frame_ref[0].astype(F32)
    ry = frame_ref[1].astype(F32)
    x = meta[2:3] * (1.0 - 2.0 * rx) + (CT - 1.0) * rx
    y = meta[3:4] * (1.0 - 2.0 * ry) + (CT - 1.0) * ry
    dx = (x + float(ox * CT)) - px
    dy = (y + float(oy * CT)) - py
    sq = dx * dx + dy * dy
    inside = sq < float(RLOC * RLOC)
    out = []
    for rate in (2.0, 4.5):
        out.append(jnp.where(inside, jnp.exp(-sq * (rate / (RLOC * RLOC))), 0.0) * meta[1:2])
    return out


def add_up(points, rows, block, frame_ref, sw_ref, wp_ref, s_ref, put_gram, put_pull):
    seen = sorted({t for p in points for t in tiles_of(p, rows)})
    place = {t: i for i, t in enumerate(seen)}
    n = padded(len(points))

    def anom(t):
        ref, ox = block(t)
        k = ORDER.index(ox) - (WIDE - ref.shape[0]) // K
        return ref[k * K : k * K + K, :]

    metas = {}
    for t in seen:
        ref, ox = block(t)
        if id(ref) not in metas:
            metas[id(ref)] = ref[ref.shape[0] - 32 :, :].astype(F32)
        k = ORDER.index(ox)
        meta = metas[id(ref)][k * META : k * META + META]
        w = point_weights(meta, frame_ref, t[0], t[1], points)
        lanes = slice(place[t] * K, place[t] * K + K)
        for g in range(2):
            sw_ref[place[t], g * n : g * n + n, :] = jnp.sqrt(w[g])
        hi, lo = split(jnp.concatenate(w, 0) * meta[0:1])
        wp_ref[0 : 2 * n, lanes] = hi
        wp_ref[2 * n : 4 * n, lanes] = lo
    anom_seen = jnp.concatenate([anom(t) for t in seen], 1)
    pull = lax.dot_general(wp_ref[...], anom_seen, NT, preferred_element_type=F32)
    put_pull(pull[0 : 2 * n] + pull[2 * n : 4 * n])

    def add_point(i):
        own = tiles_of(points[i], rows)
        for j, t in enumerate(own):
            rows_in = anom(t).astype(F32)
            for g in range(2):
                scale = sw_ref[place[t], g * n + i : g * n + i + 1, :]
                s_ref[i % SLOTS, g, :, j * K : j * K + K] = (rows_in * scale).astype(BF16)
        for g in range(2):
            s = s_ref[i % SLOTS, g, :, 0 : len(own) * K]
            put_gram(i, g, lax.dot_general(s, s, NT, preferred_element_type=F32))

    return add_point


def sum_scratch(points, rows):
    n = padded(len(points))
    seen = len({t for p in points for t in tiles_of(p, rows)})
    most = max(len(tiles_of(p, rows)) for p in points)
    return [
        pltpu.VMEM((seen, 2 * n, K), F32),
        pltpu.VMEM((4 * n, seen * K), BF16),
        pltpu.VMEM((SLOTS, 2, K, most * K), BF16),
    ]


def near_kernel(frame_ref, own_ref, other_ref, first_ref, rest_ref, pull_ref, *scratch):
    def block(t):
        return (own_ref, other_ref)[t[1]], t[0]

    def put_gram(i, g, value):
        if i < FIRST:
            first_ref[2 * i + g] = value
        else:
            rest_ref[2 * (i - FIRST) + g] = value

    def put_pull(value):
        pull_ref[...] = value

    add_point = add_up(POINTS, (0, 1), block, frame_ref, *scratch, put_gram, put_pull)
    for i in range(len(POINTS)):
        add_point(i)


def points_kernel(points, rows, batch, *refs):
    frame_ref = refs[0]
    row_refs = dict(zip(rows, refs[1:]))
    gram_ref, pull_in_ref, out_ref, sw, wp, s, g_ref, pull_ref = refs[-8:]
    n = padded(len(points))
    skip = POINTS.index(points[0])

    def block(t):
        ox, oy = t
        return row_refs[oy], -ox if oy == -1 else ox

    def put_gram(i, g, value):
        g_ref[2 * i + g] = gram_ref[2 * i + g] + value

    def put_pull(value):
        pull_ref[...] = value

    add_point = add_up(points, rows, block, frame_ref, sw, wp, s, put_gram, put_pull)
    row = lax.broadcasted_iota(jnp.int32, (K, K), 0)
    col = lax.broadcasted_iota(jnp.int32, (K, K), 1)
    eye = jnp.where(row == col, 1.0, 0.0).astype(F32)

    def steps(first):
        ids = [(p, g) for p in range(first, min(first + batch, len(points))) for g in range(2)]
        now = {}

        def gram():
            for p, g in ids[::2]:
                add_point(p)

        def scale():
            now["x"], now["norm"] = [], []
            for p, g in ids:
                system = eye + g_ref[2 * p + g] * (1.0 / (K - 1.0))
                sq = jnp.sum(jnp.sum(system * system, 0, keepdims=True), 1, keepdims=True)
                norm = jnp.sqrt(sq)
                now["norm"].append(norm)
                now["x"].append(system * (1.0 / norm))
            now["xs"] = [split(x) for x in now["x"]]

        def square(parts, out, times):
            def run():
                now[out] = [times(v, v) for v in now[parts]]

            return run

        def polynomial(x, sq, out, parts, times):
            def run():
                high = [times(parts(q), parts(C3 * v + C4 * q)) for v, q in zip(now[x], now[sq])]
                now[out] = [
                    split(C0 * eye + C1 * v + C2 * q + h) for v, q, h in zip(now[x], now[sq], high)
                ]

            return run

        def second():
            now["m"] = [mm(a, split(b)) for a, b in zip(now["xs"], now["w"])]
            now["ms"] = [split(v) for v in now["m"]]

        def inverse():
            now["i"] = [mm(a, b) for a, b in zip(now["z"], now["q"])]

        def write():
            for (p, g), z, norm in zip(ids, now["i"], now["norm"]):
                near = g * padded(len(POINTS)) + skip + p
                far = g * n + p
                pull = pull_in_ref[near : near + 1, :] + pull_ref[far : far + 1, :]
                inner = jnp.sum(z * pull, 1, keepdims=True)
                shift = jnp.sum(z * inner, 0, keepdims=True) * (1.0 / (norm * (K - 1.0)))
                out_ref[p, g] = (z * (1.0 / jnp.sqrt(norm)) + shift).astype(BF16)

        return [
            gram,
            scale,
            square("xs", "b", mm_high),
            polynomial("x", "b", "z", rounded, mm_high),
            square("z", "w", mm),
            second,
            square("ms", "c", mm),
            polynomial("m", "c", "q", split, mm),
            inverse,
            write,
        ]

    order = []
    for k, first in enumerate(range(0, len(points), batch)):
        order += [(k * LAG + j, k, step) for j, step in enumerate(steps(first))]
    for _, _, step in sorted(order, key=lambda e: e[:2]):
        step()


def specs(n, scalars=1):
    return [pl.BlockSpec(memory_space=pltpu.SMEM)] * scalars + [pl.BlockSpec(memory_space=pltpu.VMEM)] * n


def joined(kernel, rows, name, *blocks, scalars=0):
    return pl.pallas_call(
        kernel,
        out_shape=[jax.ShapeDtypeStruct((n, K), BF16) for n in rows],
        in_specs=specs(len(blocks) - scalars, scalars),
        compiler_params=pltpu.CompilerParams(vmem_limit_bytes=2 << 20),
        name=name,
    )(*blocks)


def near_sums(frame, own, other):
    n = len(POINTS)
    return pl.pallas_call(
        near_kernel,
        out_shape=[
            jax.ShapeDtypeStruct((2 * FIRST, K, K), F32),
            jax.ShapeDtypeStruct((2 * (n - FIRST), K, K), F32),
            jax.ShapeDtypeStruct((2 * padded(n), K), F32),
        ],
        in_specs=specs(2),
        scratch_shapes=sum_scratch(POINTS, (0, 1)),
        compiler_params=pltpu.CompilerParams(vmem_limit_bytes=16 << 20),
        cost_estimate=pl.CostEstimate(flops=6_000_000_000, bytes_accessed=5_000_000, transcendentals=0),
        name="near_sums",
    )(frame, own, other)


def transforms(points, rows, batch, flops, name, frame, *arrays):
    n = len(points)
    return pl.pallas_call(
        functools.partial(points_kernel, points, rows, batch),
        out_shape=jax.ShapeDtypeStruct((n, 2, K, K), BF16),
        in_specs=specs(len(arrays)),
        scratch_shapes=sum_scratch(points, rows)
        + [pltpu.VMEM((2 * n, K, K), F32), pltpu.VMEM((2 * padded(n), K), F32)],
        compiler_params=pltpu.CompilerParams(vmem_limit_bytes=28 << 20),
        cost_estimate=pl.CostEstimate(flops=flops, bytes_accessed=flops // 1000, transcendentals=0),
        name=name,
    )(frame, *arrays)


def anomalies_kernel(ens_ref, anom_ref, mean_ref):
    ones = jnp.ones((K, K), BF16)
    rows = CT * 2 * NHALF
    for i in range(CT):
        ens = ens_ref[i].reshape(rows, K)
        mean = lax.dot_general(ens, ones, NN, preferred_element_type=F32) * (1.0 / K)
        anom_ref[i] = (ens.astype(F32) - mean).astype(BF16).reshape(CT, 2 * NHALF, K)
        mean_ref[i] = mean.reshape(CT, 2 * NHALF, K)


def anomalies(ensemble):
    return pl.pallas_call(
        anomalies_kernel,
        out_shape=[
            jax.ShapeDtypeStruct(ensemble.shape, BF16),
            jax.ShapeDtypeStruct(ensemble.shape, F32),
        ],
        in_specs=specs(1, 0),
        compiler_params=pltpu.CompilerParams(vmem_limit_bytes=12 << 20),
        cost_estimate=pl.CostEstimate(flops=1_000_000_000, bytes_accessed=4_000_000, transcendentals=0),
        name="anomalies",
    )(ensemble)


def apply_kernel(frame_ref, anom_ref, mean_ref, first_ref, rest_ref, high_ref, out_ref, sum_ref):
    rx, ry, edge = frame_ref[0], frame_ref[1], frame_ref[2]

    def transform(x, y, g):
        if y == 0:
            return first_ref[x + edge * SIDE, g]
        if y < 3:
            return first_ref[y * SIDE + x, g]
        if y <= APX:
            return rest_ref[(y - 3) * SIDE + x, g]
        return high_ref[SIDE - 1 - x, g]

    frac = [(s + 0.5) / SPACING for s in range(SPACING)]
    factor = [[1.0 - f for f in frac], frac]

    def columns(x):
        at = [(i, x - (i + 1) // SPACING, (i + 1) % SPACING) for i in range(CT)]
        return [(i, factor[c][s], c == 1) for i, c, s in at if c in (0, 1)]

    def place(i, j):
        return i + rx * (CT - 1 - 2 * i), j + ry * (CT - 1 - 2 * j)

    for y in range(SIDE):
        for x in range(SIDE):
            cells = [(i, j, fi * fj, li and lj) for i, fi, li in columns(x) for j, fj, lj in columns(y)]
            for g in range(2):
                span = slice(g * NHALF, (g + 1) * NHALF)
                left = jnp.concatenate([anom_ref[(*place(i, j), span)] for i, j, _, _ in cells], 0)
                prod = lax.dot_general(left, transform(x, y, g), NT, preferred_element_type=F32)
                for c, (i, j, share, last) in enumerate(cells):
                    fresh = x == (i + 1) // SPACING and y == (j + 1) // SPACING
                    total = mean_ref[(*place(i, j), span)] if fresh else sum_ref[i, j, span]
                    total = total + prod[c * NHALF : (c + 1) * NHALF] * share
                    if last:
                        out_ref[(*place(i, j), span)] = total.astype(BF16)
                    else:
                        sum_ref[i, j, span] = total


def apply(frame, anom, mean, first, rest, high):
    return pl.pallas_call(
        apply_kernel,
        out_shape=jax.ShapeDtypeStruct(anom.shape, BF16),
        in_specs=specs(5),
        scratch_shapes=[pltpu.VMEM(anom.shape, F32)],
        compiler_params=pltpu.CompilerParams(vmem_limit_bytes=16 << 20),
        name="apply_transforms",
    )(frame, anom, mean, first, rest, high)


def moved(block, source, sizes):
    nx, ny = sizes
    pairs = []
    for x in range(nx):
        for y in range(ny):
            at = source(x, y)
            if at is not None:
                pairs.append((at[0] % nx * ny + at[1], x * ny + y))
    return lax.ppermute(block, ("gx", "gy"), pairs)


def shards(ensemble, obs_anom, obs_innov, obs_prec, obs_pos, obs_count):
    sizes = (lax.axis_size("gx"), lax.axis_size("gy"))

    def core(x, y):
        return x, y ^ 1

    def side(x, y):
        return x + 1 - 2 * ((x ^ y) & 1), y

    def second(x, y):
        return x - 2 + 4 * (((x >> 1) ^ y) & 1), y

    def beyond(x, y):
        at = y + 2 * (y & 1) - 1
        return (x, at) if 0 <= at < sizes[1] else None

    def across(x, y):
        at = y + 3 - 6 * (y & 1)
        return (x, at) if 0 <= at < sizes[1] else None

    own = pl.pallas_call(
        pack_kernel,
        out_shape=jax.ShapeDtypeStruct((ROWS, K), BF16),
        in_specs=specs(4),
        name="pack_slots",
    )(
        obs_count,
        obs_anom.reshape(K, K),
        obs_innov.reshape(1, K),
        obs_prec.reshape(1, K),
        obs_pos.reshape(2, K),
    )
    col, row = lax.axis_index("gx"), lax.axis_index("gy")
    edge = jnp.where((row == 0) | (row == sizes[1] - 1), 1, 0)
    frame = jnp.stack([(col ^ row) & 1, row & 1, edge, ((col >> 1) ^ col) & 1]).astype(jnp.int32)

    (pair,) = joined(pair_kernel, [PAIR], "pair_tiles", own, moved(own, core, sizes))
    a = moved(pair, side, sizes)
    b = moved(pair, second, sizes)
    ta = moved(a, core, sizes)
    tb = moved(b, core, sizes)
    near, next_row = joined(rows_kernel, [WIDE, WIDE], "two_rows", frame, pair, a, b, ta, tb, scalars=1)
    y1 = moved(near, beyond, sizes)
    anom, mean = anomalies(ensemble)
    gram_first, gram_rest, pull = near_sums(frame, near, next_row)
    y2 = moved(near, across, sizes)
    z1 = moved(lax.optimization_barrier((y1, pull))[0][EDGES * K :], core, sizes)
    rest = transforms(POINTS[FIRST:], (-1, 2), 12, REST, "rest_points", frame, y1, z1, gram_rest, pull)
    z2 = moved(lax.optimization_barrier((y2, rest))[0], core, sizes)
    first = transforms(POINTS[:FIRST], (-2, -1), 9, 9_000_000_000, "first_points", frame, z2, y1, gram_first, pull)
    high = moved(rest[-SIDE:], core, sizes)
    return apply(frame, anom, mean, first, rest, high)


def solution(mesh):
    placed = (
        P("gx", "gy", None, None),
        P("gx", "gy", None, None),
        P("gx", "gy", None),
        P("gx", "gy", None),
        P("gx", "gy", None, None),
        P("gx", "gy"),
    )
    return jax.shard_map(
        shards, mesh=mesh, in_specs=placed, out_specs=P("gx", "gy", None, None), check_vma=False
    )
```

```python
import functools

import jax
import jax.numpy as jnp
from jax import lax
from jax.experimental import pallas as pl
from jax.experimental.pallas import tpu as pltpu
from jax.sharding import PartitionSpec as P

K = 128
APX = 4
CT = 8
SPACING = 2
RLOC = 12
NHALF = 32
META = 4
ROWS = K + 16
PAIR = 2 * K + 16
WIDE = 5 * K + 32
ORDER = (-2, 2, -1, 0, 1)
EDGES = 2
SLOTS = 2
REST = 1_000_000
LAG = 8

NT = (((1,), (1,)), ((), ()))
NN = (((1,), (0,)), ((), ()))
F32 = jnp.float32
BF16 = jnp.bfloat16

SIDE = APX + 2
POINTS = [(a, b) for b in range(-1, APX) for a in range(-1, APX + 1)]
FIRST = 3 * SIDE


def center(a):
    return SPACING * a + (SPACING - 1) / 2.0


def least_distance(offset, point):
    return min(abs(offset * CT + s - center(point)) for s in range(CT))


def tiles_of(point, rows):
    a, b = point
    return [
        (ox, oy)
        for oy in rows
        for ox in range(-2, 3)
        if least_distance(ox, a) ** 2 + least_distance(oy, b) ** 2 < RLOC * RLOC
    ]


def split(x):
    hi = x.astype(BF16)
    lo = (x - hi.astype(F32)).astype(BF16)
    return hi, lo


def mm(a, b):
    left = jnp.concatenate([a[0], a[1]], 1)
    right = jnp.concatenate([b[0], b[1]], 1)
    right = jnp.concatenate([right, right], 0)
    out = lax.dot_general(left, right, NN, preferred_element_type=F32)
    return out[:, :K] + out[:, K:]


def rounded(x):
    return (x.astype(BF16),)


def mm_high(a, b):
    return lax.dot_general(a[0], b[0], NN, preferred_element_type=F32)


C0, C1, C2, C3, C4 = 2.25, -2.4375, 1.6875, -0.5625, 0.0625


def pack_kernel(count_ref, anom_ref, innov_ref, prec_ref, pos_ref, out_ref):
    out_ref[0:K, :] = anom_ref[...].astype(F32).T.astype(BF16)
    slot = lax.broadcasted_iota(jnp.int32, (1, K), 1)
    live = jnp.where(slot < count_ref[0, 0], prec_ref[...].astype(F32), 0.0)
    meta = jnp.concatenate(
        [innov_ref[...].astype(F32), live, pos_ref[...].astype(F32), jnp.zeros((12, K), F32)], 0
    )
    out_ref[K:ROWS, :] = meta.astype(BF16)


def pair_kernel(own_ref, other_ref, out_ref):
    out_ref[0:K, :] = own_ref[0:K, :]
    out_ref[K : 2 * K, :] = other_ref[0:K, :]
    meta = [ref[K:ROWS, :].astype(F32)[0:META] for ref in (own_ref, other_ref)]
    out_ref[2 * K : PAIR, :] = jnp.concatenate(meta + [jnp.zeros((8, K), F32)], 0).astype(BF16)


def rows_kernel(pair_ref, a_ref, b_ref, ta_ref, tb_ref, *out_refs):
    for row, out_ref in enumerate(out_refs):
        parts = [(tb_ref, 1 - row), (b_ref, row), (ta_ref, 1 - row), (pair_ref, row), (a_ref, row)]
        meta = []
        for k, (ref, at) in enumerate(parts):
            out_ref[k * K : k * K + K, :] = ref[at * K : at * K + K, :]
            meta.append(ref[2 * K : PAIR, :].astype(F32)[at * META : at * META + META])
        meta.append(jnp.zeros((12, K), F32))
        out_ref[5 * K : WIDE, :] = jnp.concatenate(meta, 0).astype(BF16)


def padded(n):
    return (n + 7) // 8 * 8


def point_weights(meta, frame_ref, ox, oy, points):
    rows = padded(len(points))
    at = lax.broadcasted_iota(jnp.int32, (rows, K), 0)
    px = jnp.zeros((rows, K), F32)
    py = px
    for i, (a, b) in enumerate(points):
        px = jnp.where(at == i, center(a), px)
        py = jnp.where(at == i, center(b), py)
    rx = frame_ref[0].astype(F32)
    ry = frame_ref[1].astype(F32)
    x = meta[2:3] * (1.0 - 2.0 * rx) + (CT - 1.0) * rx
    y = meta[3:4] * (1.0 - 2.0 * ry) + (CT - 1.0) * ry
    dx = (x + float(ox * CT)) - px
    dy = (y + float(oy * CT)) - py
    sq = dx * dx + dy * dy
    inside = sq < float(RLOC * RLOC)
    out = []
    for rate in (2.0, 4.5):
        out.append(jnp.where(inside, jnp.exp(-sq * (rate / (RLOC * RLOC))), 0.0) * meta[1:2])
    return out


def add_up(points, rows, block, frame_ref, sw_ref, wp_ref, s_ref, put_gram, put_pull):
    seen = sorted({t for p in points for t in tiles_of(p, rows)})
    place = {t: i for i, t in enumerate(seen)}
    n = padded(len(points))

    def anom(t):
        ref, ox = block(t)
        k = ORDER.index(ox) - (WIDE - ref.shape[0]) // K
        return ref[k * K : k * K + K, :]

    metas = {}
    for t in seen:
        ref, ox = block(t)
        if id(ref) not in metas:
            metas[id(ref)] = ref[ref.shape[0] - 32 :, :].astype(F32)
        k = ORDER.index(ox)
        meta = metas[id(ref)][k * META : k * META + META]
        w = point_weights(meta, frame_ref, t[0], t[1], points)
        lanes = slice(place[t] * K, place[t] * K + K)
        for g in range(2):
            sw_ref[place[t], g * n : g * n + n, :] = jnp.sqrt(w[g])
        hi, lo = split(jnp.concatenate(w, 0) * meta[0:1])
        wp_ref[0 : 2 * n, lanes] = hi
        wp_ref[2 * n : 4 * n, lanes] = lo
    anom_seen = jnp.concatenate([anom(t) for t in seen], 1)
    pull = lax.dot_general(wp_ref[...], anom_seen, NT, preferred_element_type=F32)
    put_pull(pull[0 : 2 * n] + pull[2 * n : 4 * n])

    def add_point(i):
        own = tiles_of(points[i], rows)
        for j, t in enumerate(own):
            rows_in = anom(t).astype(F32)
            for g in range(2):
                scale = sw_ref[place[t], g * n + i : g * n + i + 1, :]
                s_ref[i % SLOTS, g, :, j * K : j * K + K] = (rows_in * scale).astype(BF16)
        for g in range(2):
            s = s_ref[i % SLOTS, g, :, 0 : len(own) * K]
            put_gram(i, g, lax.dot_general(s, s, NT, preferred_element_type=F32))

    return add_point


def sum_scratch(points, rows):
    n = padded(len(points))
    seen = len({t for p in points for t in tiles_of(p, rows)})
    most = max(len(tiles_of(p, rows)) for p in points)
    return [
        pltpu.VMEM((seen, 2 * n, K), F32),
        pltpu.VMEM((4 * n, seen * K), BF16),
        pltpu.VMEM((SLOTS, 2, K, most * K), BF16),
    ]


def near_kernel(frame_ref, own_ref, other_ref, first_ref, rest_ref, pull_ref, *scratch):
    def block(t):
        return (own_ref, other_ref)[t[1]], t[0]

    def put_gram(i, g, value):
        if i < FIRST:
            first_ref[2 * i + g] = value
        else:
            rest_ref[2 * (i - FIRST) + g] = value

    def put_pull(value):
        pull_ref[...] = value

    add_point = add_up(POINTS, (0, 1), block, frame_ref, *scratch, put_gram, put_pull)
    for i in range(len(POINTS)):
        add_point(i)


def points_kernel(points, rows, batch, *refs):
    frame_ref = refs[0]
    row_refs = dict(zip(rows, refs[1:]))
    gram_ref, pull_in_ref, out_ref, sw, wp, s, g_ref, pull_ref = refs[-8:]
    n = padded(len(points))
    skip = POINTS.index(points[0])

    def block(t):
        ox, oy = t
        return row_refs[oy], -ox if oy == -1 else ox

    def put_gram(i, g, value):
        g_ref[2 * i + g] = gram_ref[2 * i + g] + value

    def put_pull(value):
        pull_ref[...] = value

    add_point = add_up(points, rows, block, frame_ref, sw, wp, s, put_gram, put_pull)
    row = lax.broadcasted_iota(jnp.int32, (K, K), 0)
    col = lax.broadcasted_iota(jnp.int32, (K, K), 1)
    eye = jnp.where(row == col, 1.0, 0.0).astype(F32)
    c0_eye = jnp.where(row == col, C0, 0.0).astype(F32)

    def steps(first):
        ids = [(p, g) for p in range(first, min(first + batch, len(points))) for g in range(2)]
        now = {}

        def gram():
            for p, g in ids[::2]:
                add_point(p)

        def scale():
            now["x"], now["norm"] = [], []
            for p, g in ids:
                system = eye + g_ref[2 * p + g] * (1.0 / (K - 1.0))
                sq = jnp.sum(jnp.sum(system * system, 0, keepdims=True), 1, keepdims=True)
                norm = jnp.sqrt(sq)
                now["norm"].append(norm)
                now["x"].append(system * (1.0 / norm))
            now["xs"] = [split(x) for x in now["x"]]

        def square(parts, out, times):
            def run():
                now[out] = [times(v, v) for v in now[parts]]

            return run

        def polynomial(x, sq, out, parts, times):
            def run():
                high = [times(parts(q), parts(C3 * v + C4 * q)) for v, q in zip(now[x], now[sq])]
                now[out] = [
                    split((c0_eye + C1 * v) + (C2 * q + h)) for v, q, h in zip(now[x], now[sq], high)
                ]

            return run

        def second():
            now["m"] = [mm(a, split(b)) for a, b in zip(now["xs"], now["w"])]
            now["ms"] = [split(v) for v in now["m"]]

        def inverse():
            now["i"] = [mm(a, b) for a, b in zip(now["z"], now["q"])]

        def write():
            for (p, g), z, norm in zip(ids, now["i"], now["norm"]):
                near = g * padded(len(POINTS)) + skip + p
                far = g * n + p
                pull = pull_in_ref[near : near + 1, :] + pull_ref[far : far + 1, :]
                inner = jnp.sum(z * pull, 1, keepdims=True)
                shift = jnp.sum(z * inner, 0, keepdims=True) * (1.0 / (norm * (K - 1.0)))
                out_ref[p, g] = (z * (1.0 / jnp.sqrt(norm)) + shift).astype(BF16)

        return [
            gram,
            scale,
            square("xs", "b", mm_high),
            polynomial("x", "b", "z", rounded, mm_high),
            square("z", "w", mm),
            second,
            square("ms", "c", mm),
            polynomial("m", "c", "q", split, mm),
            inverse,
            write,
        ]

    order = []
    for k, first in enumerate(range(0, len(points), batch)):
        order += [(k * LAG + j, k, step) for j, step in enumerate(steps(first))]
    for _, _, step in sorted(order, key=lambda e: e[:2]):
        step()


def specs(n, scalars=1):
    return [pl.BlockSpec(memory_space=pltpu.SMEM)] * scalars + [pl.BlockSpec(memory_space=pltpu.VMEM)] * n


def joined(kernel, rows, name, *blocks):
    return pl.pallas_call(
        kernel,
        out_shape=[jax.ShapeDtypeStruct((n, K), BF16) for n in rows],
        in_specs=specs(len(blocks), 0),
        compiler_params=pltpu.CompilerParams(vmem_limit_bytes=2 << 20),
        name=name,
    )(*blocks)


def near_sums(frame, own, other):
    n = len(POINTS)
    return pl.pallas_call(
        near_kernel,
        out_shape=[
            jax.ShapeDtypeStruct((2 * FIRST, K, K), F32),
            jax.ShapeDtypeStruct((2 * (n - FIRST), K, K), F32),
            jax.ShapeDtypeStruct((2 * padded(n), K), F32),
        ],
        in_specs=specs(2),
        scratch_shapes=sum_scratch(POINTS, (0, 1)),
        compiler_params=pltpu.CompilerParams(vmem_limit_bytes=16 << 20),
        cost_estimate=pl.CostEstimate(flops=6_000_000_000, bytes_accessed=5_000_000, transcendentals=0),
        name="near_sums",
    )(frame, own, other)


def transforms(points, rows, batch, flops, name, frame, *arrays):
    n = len(points)
    return pl.pallas_call(
        functools.partial(points_kernel, points, rows, batch),
        out_shape=jax.ShapeDtypeStruct((n, 2, K, K), BF16),
        in_specs=specs(len(arrays)),
        scratch_shapes=sum_scratch(points, rows)
        + [pltpu.VMEM((2 * n, K, K), F32), pltpu.VMEM((2 * padded(n), K), F32)],
        compiler_params=pltpu.CompilerParams(vmem_limit_bytes=28 << 20),
        cost_estimate=pl.CostEstimate(flops=flops, bytes_accessed=flops // 1000, transcendentals=0),
        name=name,
    )(frame, *arrays)


def anomalies_kernel(ens_ref, anom_ref, mean_ref):
    ones = jnp.ones((K, K), BF16)
    rows = CT * 2 * NHALF
    for i in range(CT):
        ens = ens_ref[i].reshape(rows, K)
        mean = lax.dot_general(ens, ones, NN, preferred_element_type=F32) * (1.0 / K)
        anom_ref[i] = (ens.astype(F32) - mean).astype(BF16).reshape(CT, 2 * NHALF, K)
        mean_ref[i] = mean.reshape(CT, 2 * NHALF, K)


def anomalies(ensemble):
    return pl.pallas_call(
        anomalies_kernel,
        out_shape=[
            jax.ShapeDtypeStruct(ensemble.shape, BF16),
            jax.ShapeDtypeStruct(ensemble.shape, F32),
        ],
        in_specs=specs(1, 0),
        compiler_params=pltpu.CompilerParams(vmem_limit_bytes=12 << 20),
        cost_estimate=pl.CostEstimate(flops=1_000_000_000, bytes_accessed=4_000_000, transcendentals=0),
        name="anomalies",
    )(ensemble)


def apply_kernel(frame_ref, anom_ref, mean_ref, first_ref, rest_ref, high_ref, out_ref, sum_ref):
    rx, ry, edge = frame_ref[0], frame_ref[1], frame_ref[2]

    def transform(x, y, g):
        if y == 0:
            return first_ref[x + edge * SIDE, g]
        if y < 3:
            return first_ref[y * SIDE + x, g]
        if y <= APX:
            return rest_ref[(y - 3) * SIDE + x, g]
        return high_ref[SIDE - 1 - x, g]

    frac = [(s + 0.5) / SPACING for s in range(SPACING)]
    factor = [[1.0 - f for f in frac], frac]

    def columns(x):
        at = [(i, x - (i + 1) // SPACING, (i + 1) % SPACING) for i in range(CT)]
        return [(i, factor[c][s], c == 1) for i, c, s in at if c in (0, 1)]

    def place(i, j):
        return i + rx * (CT - 1 - 2 * i), j + ry * (CT - 1 - 2 * j)

    for y in range(SIDE):
        for x in range(SIDE):
            cells = [(i, j, fi * fj, li and lj) for i, fi, li in columns(x) for j, fj, lj in columns(y)]
            for g in range(2):
                span = slice(g * NHALF, (g + 1) * NHALF)
                left = jnp.concatenate([anom_ref[(*place(i, j), span)] for i, j, _, _ in cells], 0)
                prod = lax.dot_general(left, transform(x, y, g), NT, preferred_element_type=F32)
                for c, (i, j, share, last) in enumerate(cells):
                    fresh = x == (i + 1) // SPACING and y == (j + 1) // SPACING
                    total = mean_ref[(*place(i, j), span)] if fresh else sum_ref[i, j, span]
                    total = total + prod[c * NHALF : (c + 1) * NHALF] * share
                    if last:
                        out_ref[(*place(i, j), span)] = total.astype(BF16)
                    else:
                        sum_ref[i, j, span] = total


def apply(frame, anom, mean, first, rest, high):
    return pl.pallas_call(
        apply_kernel,
        out_shape=jax.ShapeDtypeStruct(anom.shape, BF16),
        in_specs=specs(5),
        scratch_shapes=[pltpu.VMEM(anom.shape, F32)],
        compiler_params=pltpu.CompilerParams(vmem_limit_bytes=16 << 20),
        name="apply_transforms",
    )(frame, anom, mean, first, rest, high)


def moved(block, source, sizes):
    nx, ny = sizes
    pairs = []
    for x in range(nx):
        for y in range(ny):
            at = source(x, y)
            if at is not None:
                pairs.append((at[0] % nx * ny + at[1], x * ny + y))
    return lax.ppermute(block, ("gx", "gy"), pairs)


def shards(ensemble, obs_anom, obs_innov, obs_prec, obs_pos, obs_count):
    sizes = (lax.axis_size("gx"), lax.axis_size("gy"))

    def core(x, y):
        return x, y ^ 1

    def side(distance):
        return lambda x, y: (x + distance * (1 - 2 * ((x ^ y) & 1)), y)

    def beyond(x, y):
        at = y + 2 * (y & 1) - 1
        return (x, at) if 0 <= at < sizes[1] else None

    def across(x, y):
        at = y + 3 - 6 * (y & 1)
        return (x, at) if 0 <= at < sizes[1] else None

    own = pl.pallas_call(
        pack_kernel,
        out_shape=jax.ShapeDtypeStruct((ROWS, K), BF16),
        in_specs=specs(4),
        name="pack_slots",
    )(
        obs_count,
        obs_anom.reshape(K, K),
        obs_innov.reshape(1, K),
        obs_prec.reshape(1, K),
        obs_pos.reshape(2, K),
    )
    col, row = lax.axis_index("gx"), lax.axis_index("gy")
    edge = jnp.where((row == 0) | (row == sizes[1] - 1), 1, 0)
    frame = jnp.stack([(col ^ row) & 1, row & 1, edge]).astype(jnp.int32)

    (pair,) = joined(pair_kernel, [PAIR], "pair_tiles", own, moved(own, core, sizes))
    a = moved(pair, side(1), sizes)
    b = moved(pair, side(2), sizes)
    ta = moved(a, core, sizes)
    tb = moved(b, core, sizes)
    near, next_row = joined(rows_kernel, [WIDE, WIDE], "two_rows", pair, a, b, ta, tb)
    y1 = moved(near, beyond, sizes)
    anom, mean = anomalies(ensemble)
    gram_first, gram_rest, pull = near_sums(frame, near, next_row)
    y2 = moved(near, across, sizes)
    z1 = moved(lax.optimization_barrier((y1, pull))[0][EDGES * K :], core, sizes)
    rest = transforms(POINTS[FIRST:], (-1, 2), 12, REST, "rest_points", frame, y1, z1, gram_rest, pull)
    z2 = moved(lax.optimization_barrier((y2, rest))[0], core, sizes)
    first = transforms(POINTS[:FIRST], (-2, -1), 9, 9_000_000_000, "first_points", frame, z2, y1, gram_first, pull)
    high = moved(rest[-SIDE:], core, sizes)
    return apply(frame, anom, mean, first, rest, high)


def solution(mesh):
    placed = (
        P("gx", "gy", None, None),
        P("gx", "gy", None, None),
        P("gx", "gy", None),
        P("gx", "gy", None),
        P("gx", "gy", None, None),
        P("gx", "gy"),
    )
    return jax.shard_map(
        shards, mesh=mesh, in_specs=placed, out_specs=P("gx", "gy", None, None), check_vma=False
    )
```
